32 devices in a mesh: dp: 16 (over z, x, core), mp: 2 (over y).
Axes of the slice: x: 2, y: 2, z: 4, core: 2. Of those that a mesh axis runs over, the one named last changes fastest.
Arguments:
- tokens: bfloat16 [4096, 768], P('dp'), may hold values from -6 to 6
- w_query: bfloat16 [768, 768], P('dp', 'mp'), may hold values from -0.02734375 to 0.02734375
- w_key: bfloat16 [768, 768], P('dp', 'mp'), may hold values from -0.21875 to 0.21875
- w_value: bfloat16 [768, 768], P('dp', 'mp'), may hold values from -0.21875 to 0.21875
- w_output: bfloat16 [768, 768], P('mp', 'dp'), may hold values from -3 to 3
- bias_table: float32 [32, 12], replicated, may hold values from -6 to 6
- gain_attn: float32 [768], replicated, may hold values from 0.1 to 1.9
- gain_moe: float32 [768], replicated, may hold values from 0.1 to 1.9
- router: bfloat16 [768, 16], replicated, may hold values from -0.109375 to 0.109375
- w_in: bfloat16 [16, 768, 3072], P('dp', None, 'mp'), may hold values from -0.21875 to 0.21875
- w_out: bfloat16 [16, 3072, 768], P('dp', 'mp'), may hold values from -4 to 4
- routes: int32 [4096], P('dp'), may hold values from 0 to 15, as said below
- slots: int32 [4096], P('dp'), may hold values from 0 to 19, as said below
- buckets: int32 [511], replicated, may hold values from 0 to 31, as said below
- cotangent: bfloat16 [4096, 768], P('dp'), may hold values from -6 to 6
Outputs:
- layer_out: bfloat16 [4096, 768], P(('dp', 'mp'))
- input_grad: float32 [4096, 768], P(('dp', 'mp'))
- grad_query: float32 [768, 768], P('dp', 'mp')
- grad_key: float32 [768, 768], P('dp', 'mp')
- grad_value: float32 [768, 768], P('dp', 'mp')
- grad_output: float32 [768, 768], P('mp', 'dp')
- grad_table: float32 [32, 12], replicated
- grad_gain_attn: float32 [768], replicated
- grad_gain_moe: float32 [768], replicated
- grad_router: float32 [768, 16], replicated
- grad_w_in: float32 [16, 768, 3072], P('dp', None, 'mp')
- grad_w_out: float32 [16, 3072, 768], P('dp', 'mp')
The draws below stay inside these ranges and needn't reach their ends.
Inputs may be any that keep to these rules, and one draw needn't show every extreme that they name: `routes`: in each sequence of 256 tokens no expert is named by more than 20 tokens, and one expert, the same in all sequences, is named by exactly 20. Within each sequence the pairs (routes, slots) are all different. `buckets`: entry k - q + 255 is the bucket of key k seen from query q.
All inputs are finite; a program needn't handle non-finite values.
Results may differ from the reference program's by a relative error of at most 0.02.
Values may be sent and summed in bfloat16 or wider, within the bound.
A program may use at most 128 MiB of HBM per device.

```python
import jax
import jax.numpy as jnp
from jax import lax

D = 768
HEADS = 12
HEAD_DIM = 64
FF = 3072
BUCKETS = 32
SEQ = 256
EXPERTS = 16
CAP = 20
TOKENS = 4096
N_MP = 2


def routing_ids(key):
    count_seq = TOKENS // SEQ
    slot_total = EXPERTS * CAP
    chosen = jax.random.randint(jax.random.fold_in(key, 11), (), 0, EXPERTS)
    first_key = jax.random.fold_in(key, 12)
    second_key = jax.random.fold_in(key, 13)

    def one_sequence(block_index):
        shuffled = jax.random.permutation(jax.random.fold_in(first_key, block_index), slot_total)
        later_rank = (shuffled // CAP != chosen).astype(jnp.int32)
        ordering = jnp.argsort(later_rank, stable=True)
        picked = shuffled[ordering][:SEQ]
        mixing = jax.random.permutation(jax.random.fold_in(second_key, block_index), SEQ)
        return picked[mixing]
    return jax.vmap(one_sequence)(jnp.arange(count_seq, dtype=jnp.int32)).reshape(-1).astype(jnp.int32)


def draw_routes(key, part):
    flat_ids = routing_ids(key)
    return flat_ids // CAP


def draw_slots(key, part):
    flat_ids = routing_ids(key)
    return flat_ids % CAP


def draw_buckets(key, part):
    key = jax.random.fold_in(key, 5)
    breakpoints = jax.random.randint(key, (7,), 9, SEQ)
    offsets = jnp.arange(2 * SEQ - 1, dtype=jnp.int32) - (SEQ - 1)
    distance = jnp.abs(offsets)
    far_bucket = 8 + jnp.sum((distance[:, None] >= breakpoints[None, :]).astype(jnp.int32), axis=1)
    near_far = jnp.where(distance < 8, distance, far_bucket)
    return (near_far + jnp.where(offsets > 0, 16, 0)).astype(jnp.int32)


def block_scale(stream_key, extent, split, least, high):
    def one(axis_at, parts):
        heights = jax.random.uniform(jax.random.fold_in(jax.random.fold_in(stream_key, 6), axis_at), (parts,), jnp.float32, least / len(split), high / len(split))
        return jnp.repeat(jnp.exp(heights), extent[axis_at] // parts).reshape((-1,) + (1,) * (len(extent) - axis_at - 1))

    factor_of = one(*split[0])
    for cut in split[1:]:
        factor_of = factor_of * one(*cut)
    return factor_of


def centred(own_key, dims, width, limit, cuts=(), kind=jnp.bfloat16):
    loudness = block_scale(own_key, dims, cuts, -0.22, 0.18) if cuts else 1.0
    drawn = jax.random.normal(own_key, dims, jnp.float32) * width * loudness
    return jnp.minimum(jnp.maximum(drawn, -limit), limit).astype(kind)


def setup_inputs(seed: int = 0) -> dict:
    splits = jax.random.split(jax.random.key(seed), 16)
    tokens = centred(splits[0], (TOKENS, D), 1.0, 6.0, ((0, 16),))
    w_query = centred(splits[1], (D, HEADS * HEAD_DIM), ((D * HEAD_DIM) ** -0.5), 0.02734375, ((0, 16), (1, 2)))
    w_key = centred(splits[2], (D, HEADS * HEAD_DIM), D ** -0.5, 0.21875, ((0, 16), (1, 2)))
    w_value = centred(splits[3], (D, HEADS * HEAD_DIM), D ** -0.5, 0.21875, ((0, 16), (1, 2)))
    w_output = centred(splits[4], (HEADS * HEAD_DIM, D), 0.5, 3.0, ((0, 2), (1, 16)))
    bias_table = centred(splits[5], (BUCKETS, HEADS), 1.0, 6.0, (), jnp.float32)
    gain_attn = jnp.clip(1.0 + 0.18 * jax.random.normal(splits[6], (D,), jnp.float32), 0.1, 1.9)
    gain_moe = jnp.clip(1.0 + 0.18 * jax.random.normal(splits[7], (D,), jnp.float32), 0.1, 1.9)
    router = centred(splits[8], (D, EXPERTS), (0.5 * D ** -0.5), 0.109375)
    w_in = centred(splits[9], (EXPERTS, D, FF), D ** -0.5, 0.21875, ((0, 16), (2, 2)))
    w_out = centred(splits[10], (EXPERTS, FF, D), (2.5 * EXPERTS * FF ** -0.5), 4.0, ((0, 16), (1, 2)))
    routes = draw_routes(jax.random.fold_in(splits[15], 71), 0)
    slots = draw_slots(jax.random.fold_in(splits[15], 71), 0)
    buckets = draw_buckets(jax.random.fold_in(splits[15], 71), 0)
    cotangent = centred(splits[14], (TOKENS, D), 1.0, 6.0, ((0, 16),))
    return {"tokens": tokens, "w_query": w_query, "w_key": w_key, "w_value": w_value, "w_output": w_output, "bias_table": bias_table, "gain_attn": gain_attn, "gain_moe": gain_moe, "router": router, "w_in": w_in, "w_out": w_out, "routes": routes, "slots": slots, "buckets": buckets, "cotangent": cotangent}


EPS = 1e-06
HIGH = lax.Precision.HIGHEST

@jax.custom_vjp
def low(v):
    return lax.optimization_barrier(v.astype(jnp.bfloat16)).astype(jnp.float32)

@jax.custom_vjp
def low_back(v):
    return v

def low_keep(v):
    return (low(v), None)

def low_pass(kept, grad):
    return (grad,)

def back_keep(v):
    return (v, None)

def back_low(kept, grad):
    return (low(grad),)
low.defvjp(low_keep, low_pass)
low_back.defvjp(back_keep, back_low)

def rounded_both(values):
    return low_back(low(values))

def rms_norm(values, gains):
    return values * lax.rsqrt(lax.optimization_barrier(jnp.mean(values * values, axis=-1, keepdims=True)) + EPS) * gains

def sequence_layer(inputs, w_query, w_key, w_value, w_output, bias_table, gain_attn, gain_moe, router, w_in, w_out, routes, slots, buckets):
    length, model_width = inputs.shape
    head_count = bias_table.shape[1]
    head_size = w_query.shape[1] // head_count
    normed_attn = low(rms_norm(inputs, gain_attn))
    queries = rounded_both(jnp.dot(normed_attn, w_query, precision=HIGH)).reshape(length, head_count, head_size)
    keys_all = rounded_both(jnp.dot(normed_attn, w_key, precision=HIGH)).reshape(length, head_count, head_size)
    values = rounded_both(jnp.dot(normed_attn, w_value, precision=HIGH)).reshape(length, head_count, head_size)
    relative = jnp.arange(length)[None, :] - jnp.arange(length)[:, None] + length - 1
    bias = jnp.transpose(bias_table[buckets[relative]], (2, 0, 1))
    scores = low_back(jnp.einsum('qhd,khd->hqk', queries, keys_all, precision=HIGH)) + bias
    chances = low(jax.nn.softmax(scores, axis=-1))
    context = rounded_both(jnp.einsum('hqk,khd->qhd', chances, values, precision=HIGH).reshape(length, head_count * head_size))
    pieces = jnp.einsum('sgk,gkd->gsd', context.reshape(length, N_MP, -1), w_output.reshape(N_MP, -1, model_width), precision=HIGH)
    attended = low_back(lax.optimization_barrier(jnp.sum(low(pieces), axis=0)))
    residual = inputs + attended
    normed_moe = low(rms_norm(residual, gain_moe))
    logits = low_back(jnp.dot(normed_moe, router, precision=HIGH))
    chance_all = jax.nn.softmax(logits, axis=-1)
    gates = jnp.take_along_axis(chance_all, routes[:, None], axis=1)[:, 0]
    experts = router.shape[1]
    target = routes * CAP + slots
    slotted = low_back(jnp.zeros((experts * CAP, model_width), jnp.float32).at[target].set(normed_moe)).reshape(experts, CAP, model_width)
    hidden_pre = low_back(jnp.einsum('ecd,edf->ecf', slotted, w_in, precision=HIGH))
    hidden = low(jax.nn.gelu(hidden_pre, approximate=False))
    inner = w_in.shape[2] // N_MP
    groups = jnp.einsum('ecgf,egfd->gecd', hidden.reshape(experts, CAP, N_MP, inner), w_out.reshape(experts, N_MP, inner, model_width), precision=HIGH)
    expert_rows = rounded_both(lax.optimization_barrier(jnp.sum(low(groups), axis=0))).reshape(experts * CAP, model_width)
    return residual + gates[:, None] * expert_rows[target]

def reference(tokens, w_query, w_key, w_value, w_output, bias_table, gain_attn, gain_moe, router, w_in, w_out, routes, slots, buckets, cotangent):
    params = (w_query.astype(jnp.float32), w_key.astype(jnp.float32), w_value.astype(jnp.float32), w_output.astype(jnp.float32), bias_table, gain_attn, gain_moe, router.astype(jnp.float32), w_in.astype(jnp.float32), w_out.astype(jnp.float32))
    model_width = tokens.shape[1]
    count_seq = tokens.shape[0] // SEQ
    inputs_all = tokens.astype(jnp.float32).reshape(count_seq, SEQ, model_width)
    grads_all = cotangent.astype(jnp.float32).reshape(count_seq, SEQ, model_width)

    def one_sequence(running, items):
        inputs, route_ids, slot_ids, gradient = items

        def forward(inputs_seq, *weights):
            return sequence_layer(inputs_seq, *weights, route_ids, slot_ids, buckets)
        result, pull_back = jax.vjp(forward, inputs, *params)
        pulled = pull_back(gradient)
        running = tuple((earlier + update for earlier, update in zip(running, pulled[1:])))
        return (running, (result.astype(jnp.bfloat16), pulled[0]))
    initial = tuple((jnp.zeros_like(weight) for weight in params))
    totals, (layer_out, input_grad) = lax.scan(one_sequence, initial, (inputs_all, routes.reshape(count_seq, SEQ), slots.reshape(count_seq, SEQ), grads_all))
    return (layer_out.reshape(-1, model_width), input_grad.reshape(-1, model_width), totals[0], totals[1], totals[2], totals[3], totals[4], totals[5], totals[6], totals[7], totals[8], totals[9])
```

```python
import jax
import jax.numpy as jnp
from jax import lax
from jax.experimental import pallas as pl
from jax.experimental.pallas import tpu as pltpu
from jax.sharding import PartitionSpec as P

HEAD_DIM = 64


EPS = 1e-06
query_rows = 512


def in_blocks(array, dim, count):
    lengths = array.shape
    tiles = array.reshape(*lengths[:dim], count, lengths[dim] // count, *lengths[dim + 1 :])
    return jnp.moveaxis(tiles, dim, 0)


def sum_at_owner(array, axis, dim):
    count = lax.axis_size(axis)
    tiles = lax.all_to_all(in_blocks(array, dim, count), axis, 0, 0, tiled=True)
    return jnp.sum(tiles.astype(jnp.float32), axis=0)


def in_one_piece(arrays, axis, dim, along):
    ends, at = ([], 0)
    for a in arrays[:-1]:
        at += a.shape[along]
        ends.append(at)
    both = jnp.concatenate(arrays, axis=along)
    return tuple(jnp.split(sum_at_owner(both, axis, dim), ends, axis=along))


def normalize(inputs, gains):
    inverse = lax.rsqrt(jnp.mean(inputs * inputs, axis=-1, keepdims=True) + EPS)
    return (inputs * inverse * gains, inverse)


def norm_backward(inputs, inverse, gains, gradient):
    unit_rows = inputs * inverse
    scaled = gradient * gains
    return inverse * (scaled - unit_rows * jnp.mean(unit_rows * scaled, axis=-1, keepdims=True))


def offset_band(offset_bias, row_count, key_count):
    head_count = offset_bias.shape[0]
    window = offset_bias
    window = jnp.concatenate([window, jnp.zeros((head_count, 1), window.dtype)], axis=1)
    turned = jnp.concatenate([window[:, row_count - 1 :], window[:, : row_count - 1]], axis=1)
    span = row_count + key_count - 1
    repeated = jnp.tile(turned, (1, row_count))[:, : row_count * span]
    return repeated.reshape(head_count, row_count, span)[:, :, :key_count]


def band_sums(gradient, row_count, key_count):
    head_count = gradient.shape[0]
    padded = jnp.concatenate(
        [jnp.zeros((head_count, row_count, row_count), gradient.dtype), gradient], axis=2
    )
    flattened = jnp.concatenate(
        [padded.reshape(head_count, -1), jnp.zeros((head_count, row_count), gradient.dtype)], axis=1
    )
    skewed = flattened.reshape(head_count, row_count, row_count + key_count + 1)
    return jnp.sum(skewed, axis=1)[:, 1 : row_count + key_count]


def local(
    tokens,
    w_query,
    w_key,
    w_value,
    w_output,
    bias_table,
    gain_attn,
    gain_moe,
    router,
    w_in,
    w_out,
    routes,
    slots,
    buckets,
    cotangent,
):
    length, model_width = tokens.shape
    mp_count = lax.axis_size("mp")
    mp_rank = lax.axis_index("mp")
    own_rows = length // mp_count
    own_first = mp_rank * own_rows
    experts = router.shape[1]
    capacity = (5 * length + 4 * experts - 1) // (4 * experts)
    head_width = w_query.shape[1]
    head_count = head_width // HEAD_DIM
    row_block = min(query_rows, length)
    block_count = length // row_block
    block_starts = jnp.arange(block_count, dtype=jnp.int32) * row_block

    def own_slice(array):
        return lax.dynamic_slice_in_dim(array, own_first, own_rows, 0)

    inputs = tokens.astype(jnp.float32)
    normed_float, inverse_attn = normalize(inputs, gain_attn)
    normed_attn = normed_float.astype(jnp.bfloat16)
    full_query, full_key, full_value, full_output = (
        lax.all_gather(w_query, "dp", axis=0, tiled=True),
        lax.all_gather(w_key, "dp", axis=0, tiled=True),
        lax.all_gather(w_value, "dp", axis=0, tiled=True),
        lax.all_gather(w_output, "dp", axis=1, tiled=True),
    )
    w_joint = jnp.concatenate([full_query, full_key, full_value], axis=1)
    projected = jnp.dot(normed_attn, w_joint, preferred_element_type=jnp.float32).astype(
        jnp.bfloat16
    )
    queries = projected[:, :head_width].reshape(length, head_count, HEAD_DIM)
    keys_all = projected[:, head_width : 2 * head_width].reshape(length, head_count, HEAD_DIM)
    values = projected[:, 2 * head_width :].reshape(length, head_count, HEAD_DIM)
    bucket_hot = (
        buckets[:, None] == jnp.arange(bias_table.shape[0], dtype=jnp.int32)[None, :]
    ).astype(jnp.float32)
    table_heads = lax.dynamic_slice_in_dim(bias_table, mp_rank * head_count, head_count, 1)
    offset_bias = jnp.einsum("ob,bh->ho", bucket_hot, table_heads, precision=lax.Precision.HIGHEST)

    def attend_block(first_row):
        scores = jnp.einsum(
            "qhd,khd->hqk", queries, keys_all, preferred_element_type=jnp.float32
        ) + offset_band(offset_bias, row_block, length)
        peak_score = jnp.max(scores, axis=-1, keepdims=True)
        weights = jnp.exp(scores - peak_score)
        summed = jnp.sum(weights, axis=-1, keepdims=True)
        chances = (weights / summed).astype(jnp.bfloat16)
        context_rows = jnp.einsum(
            "hqk,khd->qhd", chances, values, preferred_element_type=jnp.float32
        )
        return (context_rows.astype(jnp.bfloat16), (peak_score + jnp.log(summed))[:, :, 0])

    context_blocks, log_totals = lax.map(attend_block, block_starts)
    context = context_blocks.reshape(length, head_width)
    partial_attn = jnp.dot(context, full_output, preferred_element_type=jnp.float32)
    attended = lax.psum(partial_attn.astype(jnp.bfloat16), "mp").astype(jnp.float32)
    residual = inputs + attended
    moe_float, inverse_moe = normalize(residual, gain_moe)
    normed_moe = moe_float.astype(jnp.bfloat16)
    logits = jnp.dot(normed_moe, router, preferred_element_type=jnp.float32)
    chance_all = jax.nn.softmax(logits, axis=-1)
    route_hot = (routes[:, None] == jnp.arange(experts, dtype=jnp.int32)[None, :]).astype(
        jnp.float32
    )
    gates = jnp.sum(chance_all * route_hot, axis=1)
    target = routes * capacity + slots
    slotted = (
        jnp.zeros((experts * capacity, model_width), jnp.bfloat16)
        .at[target]
        .set(normed_moe)
        .reshape(experts, capacity, model_width)
    )
    arrived = lax.all_to_all(slotted, "dp", split_axis=0, concat_axis=0, tiled=True)
    expert_input = arrived.reshape(-1, model_width)
    hidden_pre = jnp.dot(expert_input, w_in[0], preferred_element_type=jnp.float32)
    gelu_value, gelu_back = jax.vjp(lambda inner: jax.nn.gelu(inner, approximate=False), hidden_pre)
    hidden = gelu_value.astype(jnp.bfloat16)
    partial_out = jnp.dot(hidden, w_out[0], preferred_element_type=jnp.float32).reshape(
        arrived.shape
    )
    summed_out = lax.psum(partial_out.astype(jnp.bfloat16), "mp")
    returned = lax.all_to_all(summed_out, "dp", split_axis=0, concat_axis=0, tiled=True)
    expert_rows = returned.reshape(experts * capacity, model_width)[target].astype(jnp.float32)
    layer_full = residual + gates[:, None] * expert_rows
    layer_out = own_slice(layer_full).astype(jnp.bfloat16)
    gradient = cotangent.astype(jnp.float32)
    grad_gates = jnp.sum(gradient * expert_rows, axis=1)
    grad_rows = (gates[:, None] * gradient).astype(jnp.bfloat16)
    grad_slotted = (
        jnp.zeros((experts * capacity, model_width), jnp.bfloat16)
        .at[target]
        .set(grad_rows)
        .reshape(experts, capacity, model_width)
    )
    grad_arrived = lax.all_to_all(grad_slotted, "dp", split_axis=0, concat_axis=0, tiled=True)
    grad_expert = grad_arrived.reshape(-1, model_width)
    grad_hidden = jnp.einsum("rd,fd->rf", grad_expert, w_out[0], preferred_element_type=jnp.float32)
    grad_pre = gelu_back(grad_hidden)[0].astype(jnp.bfloat16)
    grad_w_out = jnp.einsum("rf,rd->fd", hidden, grad_expert, preferred_element_type=jnp.float32)[
        None
    ]
    grad_w_in = jnp.einsum("rd,rf->df", expert_input, grad_pre, preferred_element_type=jnp.float32)[
        None
    ]
    partial_back = jnp.einsum(
        "rf,df->rd", grad_pre, w_in[0], preferred_element_type=jnp.float32
    ).reshape(arrived.shape)
    grad_input_slots = lax.psum(partial_back.astype(jnp.bfloat16), "mp")
    grad_sent = lax.all_to_all(grad_input_slots, "dp", split_axis=0, concat_axis=0, tiled=True)
    grad_normed = grad_sent.reshape(experts * capacity, model_width)[target].astype(jnp.float32)
    grad_logits = (grad_gates[:, None] * gates[:, None] * (route_hot - chance_all)).astype(
        jnp.bfloat16
    )
    grad_normed = grad_normed + jnp.einsum(
        "se,de->sd", grad_logits, router, preferred_element_type=jnp.float32
    )
    grad_residual = gradient + norm_backward(residual, inverse_moe, gain_moe, grad_normed)
    grad_gain_moe = jnp.sum(own_slice(grad_normed) * own_slice(residual * inverse_moe), axis=0)
    grad_router = jnp.einsum(
        "sd,se->de",
        own_slice(normed_moe),
        own_slice(grad_logits),
        preferred_element_type=jnp.float32,
    )
    grad_attended = grad_residual.astype(jnp.bfloat16)
    grad_output = jnp.einsum(
        "sk,sd->kd", context, grad_attended, preferred_element_type=jnp.float32
    )
    grad_context = (
        jnp.einsum("sd,kd->sk", grad_attended, full_output, preferred_element_type=jnp.float32)
        .astype(jnp.bfloat16)
        .reshape(length, head_count, HEAD_DIM)
    )

    def back_block(running, items):
        first_row, log_total = items
        grad_keys, grad_values, grad_offsets = running
        scores = jnp.einsum(
            "qhd,khd->hqk", queries, keys_all, preferred_element_type=jnp.float32
        ) + offset_band(offset_bias, row_block, length)
        chances = jnp.exp(scores - log_total[:, :, None])
        grad_chances = jnp.einsum(
            "qhd,khd->hqk", grad_context, values, preferred_element_type=jnp.float32
        )
        grad_scores = chances * (
            grad_chances - jnp.sum(grad_chances * chances, axis=-1, keepdims=True)
        )
        grad_offsets = grad_offsets + band_sums(grad_scores, row_block, length)
        grad_low = grad_scores.astype(jnp.bfloat16)
        grad_queries = jnp.einsum(
            "hqk,khd->qhd", grad_low, keys_all, preferred_element_type=jnp.float32
        )
        grad_keys = grad_keys + jnp.einsum(
            "hqk,qhd->khd", grad_low, queries, preferred_element_type=jnp.float32
        )
        grad_values = grad_values + jnp.einsum(
            "hqk,qhd->khd",
            chances.astype(jnp.bfloat16),
            grad_context,
            preferred_element_type=jnp.float32,
        )
        return ((grad_keys, grad_values, grad_offsets), grad_queries.astype(jnp.bfloat16))

    zero_heads = jnp.zeros((length, head_count, HEAD_DIM), jnp.float32)
    zero_offsets = jnp.zeros((head_count, 2 * length - 1), jnp.float32)
    (grad_keys, grad_values, grad_offsets), grad_queries = lax.scan(
        back_block, (zero_heads, zero_heads, zero_offsets), (block_starts, log_totals)
    )
    grad_joint = jnp.concatenate(
        [
            grad_queries.reshape(length, head_width),
            grad_keys.astype(jnp.bfloat16).reshape(length, head_width),
            grad_values.astype(jnp.bfloat16).reshape(length, head_width),
        ],
        axis=1,
    )
    grad_weights = jnp.einsum(
        "sd,sk->dk", normed_attn, grad_joint, preferred_element_type=jnp.float32
    )
    grad_query, grad_key, grad_value, grad_out_proj = (
        *in_one_piece(
            (
                grad_weights[:, :head_width].astype(jnp.bfloat16),
                grad_weights[:, head_width : 2 * head_width].astype(jnp.bfloat16),
                grad_weights[:, 2 * head_width :].astype(jnp.bfloat16),
            ),
            "dp",
            0,
            1,
        ),
        sum_at_owner(grad_output.astype(jnp.bfloat16), "dp", 1),
    )
    own_grad_attn = lax.psum_scatter(
        jnp.einsum("sk,dk->sd", grad_joint, w_joint, preferred_element_type=jnp.float32).astype(
            jnp.bfloat16
        ),
        "mp",
        scatter_dimension=0,
        tiled=True,
    ).astype(jnp.float32)
    own_inputs = own_slice(inputs)
    own_inverse = own_slice(inverse_attn)
    input_grad = own_slice(grad_residual) + norm_backward(
        own_inputs, own_inverse, gain_attn, own_grad_attn
    )
    grad_gain_attn = jnp.sum(own_grad_attn * own_inputs * own_inverse, axis=0)
    table_part = jnp.einsum("ob,ho->bh", bucket_hot, grad_offsets, precision=lax.Precision.HIGHEST)
    table_full = lax.dynamic_update_slice_in_dim(
        jnp.zeros(bias_table.shape, jnp.float32), table_part, mp_rank * head_count, 1
    )
    grad_table, gain_attn_total, gain_moe_total, router_total = lax.psum(
        (table_full, grad_gain_attn, grad_gain_moe, grad_router), ("dp", "mp")
    )
    return (
        layer_out,
        input_grad,
        grad_query,
        grad_key,
        grad_value,
        grad_out_proj,
        grad_table,
        gain_attn_total,
        gain_moe_total,
        router_total,
        grad_w_in,
        grad_w_out,
    )


BF = jnp.bfloat16
F32 = jnp.float32
MESH = pl.DeviceIdType.MESH
VM = pl.BlockSpec(memory_space=pltpu.VMEM)
SLAB = 48


def params(collective_id=None):
    if collective_id is None:
        return pltpu.CompilerParams(vmem_limit_bytes=48 * 2**20)
    return pltpu.CompilerParams(
        vmem_limit_bytes=48 * 2**20, collective_id=collective_id, has_side_effects=True
    )


def dot(a, b, dims):
    return lax.dot_general(a, b, ((dims[:1], dims[1:]), ((), ())), preferred_element_type=F32)


def greet(devices):
    barrier = pltpu.get_barrier_semaphore()
    for device in devices:
        pl.semaphore_signal(barrier, inc=1, device_id=device, device_id_type=MESH)
    pl.semaphore_wait(barrier, len(devices))


def remote(src, dst, send, recv, device):
    return pltpu.make_async_remote_copy(
        src_ref=src, dst_ref=dst, send_sem=send, recv_sem=recv, device_id=device, device_id_type=MESH
    )


def place():
    dp = lax.axis_index("dp")
    return dp, lax.axis_index("mp"), dp // 4, (dp // 2) % 2, dp % 2


def gather_kernel(own_ref, out_ref, own_sem, send, recv):
    dp, mp, z, x, core = place()
    sib = dp + 1 - 2 * core
    across = dp + 2 - 4 * x
    barrier = pltpu.get_barrier_semaphore()
    for other in (sib, across):
        pl.semaphore_signal(barrier, inc=1, device_id=(other, mp), device_id_type=MESH)

    @pl.when(z > 0)
    def _():
        pl.semaphore_signal(barrier, inc=1, device_id=(dp - 4, mp), device_id_type=MESH)

    @pl.when(z < 3)
    def _():
        pl.semaphore_signal(barrier, inc=1, device_id=(dp + 4, mp), device_id_type=MESH)

    pl.semaphore_wait(barrier, 2 + jnp.minimum(z, 1) + jnp.minimum(3 - z, 1))

    def block(b):
        return out_ref.at[:, pl.ds(pl.multiple_of(b * 48, 48), 48), :]

    def copy(b, way, device, src=None):
        return remote(
            block(b) if src is None else src, block(b), send.at[way, b], recv.at[b], (device, mp)
        )

    own = pltpu.make_async_copy(own_ref, block(dp), own_sem)
    own.start()

    def spread(b, src, up, down):
        @pl.when(jnp.logical_and(up, z < 3))
        def _():
            copy(b, 0, dp + 4, src).start()

        @pl.when(jnp.logical_and(down, z > 0))
        def _():
            copy(b, 1, dp - 4, src).start()

        copy(b, 2, across, src).start()
        copy(b, 3, sib, src).start()

    spread(dp, own_ref, True, True)
    for s in (1, 2, 3):

        @pl.when(z - s >= 0)
        def _():
            b = dp - 4 * s
            copy(b, 0, sib).wait_recv()
            spread(b, None, True, False)

        @pl.when(z + s <= 3)
        def _():
            b = dp + 4 * s
            copy(b, 0, sib).wait_recv()
            spread(b, None, False, True)

    for s in range(4):
        for sign in (1, -1) if s else (1,):

            @pl.when(jnp.logical_and(z + sign * s >= 0, z + sign * s <= 3))
            def _():
                b = across + 4 * s * sign
                copy(b, 0, sib).wait_recv()
                copy(b, 3, sib).start()

    for zz in range(4):
        for xx in range(2):
            copy(zz * 4 + xx * 2 + 1 - core, 3, sib).wait_recv()
    own.wait()
    for zz in range(4):
        b = zz * 4 + x * 2 + core

        @pl.when(jnp.logical_and(zz <= z, z < 3))
        def _():
            copy(b, 0, sib).wait_send()

        @pl.when(jnp.logical_and(zz >= z, z > 0))
        def _():
            copy(b, 1, sib).wait_send()

        copy(b, 2, sib).wait_send()
        copy(b, 3, sib).wait_send()
        copy(zz * 4 + (1 - x) * 2 + core, 3, sib).wait_send()


def gather_weights(own):
    return pl.pallas_call(
        gather_kernel,
        out_shape=jax.ShapeDtypeStruct((own.shape[0], 768, own.shape[2]), BF),
        in_specs=[VM],
        out_specs=VM,
        scratch_shapes=[
            pltpu.SemaphoreType.DMA,
            pltpu.SemaphoreType.DMA((4, 16)),
            pltpu.SemaphoreType.DMA((16,)),
        ],
        compiler_params=params(1),
    )(own)


def forward_kernel(heads, tokens_ref, gain_ref, w_ref, off_ref, part_ref, normed_ref, qkv_ref, ctx_ref, p_ref):
    x = tokens_ref[...].astype(F32)
    normed = normalize(x, gain_ref[...])[0].astype(BF)
    normed_ref[...] = normed
    for j in range(3):
        qkv_ref[j] = dot(normed, w_ref[j], (1, 0)).astype(BF)
    length = x.shape[0]
    for h in range(heads):
        cols = slice(h * HEAD_DIM, (h + 1) * HEAD_DIM)
        row = jnp.broadcast_to(off_ref[h : h + 1, :], (length, 2 * length))
        bias = pltpu.roll(row, length + 1, 1, stride=1, stride_axis=0)[:, :length]
        scores = dot(qkv_ref[0, :, cols], qkv_ref[1, :, cols], (1, 1)) + bias
        weights = jnp.exp(scores - jnp.max(scores, axis=-1, keepdims=True))
        chances = weights / jnp.sum(weights, axis=-1, keepdims=True)
        p_ref[h] = chances
        ctx_ref[:, cols] = dot(chances.astype(BF), qkv_ref[2, :, cols], (1, 0)).astype(BF)
    part_ref[...] = dot(ctx_ref[...], w_ref[3], (1, 1)).astype(BF)


def backward_kernel(heads, g_ref, normed_ref, w_ref, qkv_ref, ctx_ref, p_ref, gw_ref, ga_ref, goff_ref, gc_ref, gj_ref):
    length = g_ref.shape[0]
    grad = g_ref[...]
    gw_ref[3] = dot(grad, ctx_ref[...], (0, 0)).astype(BF)
    gc_ref[...] = dot(grad, w_ref[3], (1, 0)).astype(BF)
    flip = (
        lax.broadcasted_iota(jnp.int32, (length, length), 0)
        + lax.broadcasted_iota(jnp.int32, (length, length), 1)
        == length - 1
    ).astype(F32).astype(BF)
    zeros = jnp.zeros((length, length), F32)
    goff_ref[...] = jnp.zeros_like(goff_ref)
    for h in range(heads):
        cols = slice(h * HEAD_DIM, (h + 1) * HEAD_DIM)
        chances = p_ref[h]
        gctx = gc_ref[:, cols]
        grad_chances = dot(gctx, qkv_ref[2, :, cols], (1, 1))
        grad_scores = chances * (
            grad_chances - jnp.sum(grad_chances * chances, axis=-1, keepdims=True)
        )
        high = grad_scores.astype(BF)
        rest = (grad_scores - high.astype(F32)).astype(BF)
        flipped = dot(flip, high, (1, 0)) + dot(flip, rest, (1, 0))
        skewed = pltpu.roll(
            jnp.concatenate([flipped, zeros], axis=1), 0, 1, stride=1, stride_axis=0
        )
        goff_ref[h : h + 1, :] = jnp.sum(skewed, axis=0, keepdims=True)
        gj_ref[0, :, cols] = dot(high, qkv_ref[1, :, cols], (1, 0)).astype(BF)
        gj_ref[1, :, cols] = dot(high, qkv_ref[0, :, cols], (0, 0)).astype(BF)
        gj_ref[2, :, cols] = dot(chances.astype(BF), gctx, (0, 0)).astype(BF)
    total = None
    for j in range(3):
        gw_ref[j] = dot(normed_ref[...], gj_ref[j], (0, 0)).astype(BF)
        term = dot(gj_ref[j], w_ref[j], (1, 1))
        total = term if total is None else total + term
    ga_ref[...] = total.astype(BF)


def pair_kernel(a_ref, o_ref, got, send, recv):
    dp, mp = lax.axis_index("dp"), lax.axis_index("mp")
    greet([(dp, 1 - mp)])
    c = remote(a_ref, got, send, recv, (dp, 1 - mp))
    c.start()
    c.wait()
    o_ref[...] = a_ref[...].astype(F32) + got[...].astype(F32)


def pair_sum(a):
    return pl.pallas_call(
        pair_kernel,
        out_shape=jax.ShapeDtypeStruct(a.shape, F32),
        in_specs=[VM],
        out_specs=VM,
        scratch_shapes=[pltpu.VMEM(a.shape, a.dtype), pltpu.SemaphoreType.DMA, pltpu.SemaphoreType.DMA],
        compiler_params=params(2),
    )(a)


def dispatch_kernel(slab_ref, out_ref, own_sem, send, recv, ysend, yrecv):
    dp, mp = lax.axis_index("dp"), lax.axis_index("mp")
    half = slab_ref.shape[2]
    greet([((dp + k) % 16, mp) for k in range(1, 16)] + [(dp, 1 - mp)])

    def spot(s, m):
        return out_ref.at[s, :, pl.ds(pl.multiple_of(m * half, half), half)]

    own = pltpu.make_async_copy(slab_ref.at[dp], spot(dp, mp), own_sem)
    own.start()

    def cross(k):
        s = (dp + 16 - k) % 16
        src = slab_ref.at[dp] if k == 0 else spot(s, mp)
        return remote(src, spot(s, mp), ysend.at[k], yrecv.at[k], (dp, 1 - mp))

    def direct(k):
        to = (dp + k) % 16
        return remote(slab_ref.at[to], spot(dp, mp), send.at[k], recv.at[k], (to, mp))

    for k in range(1, 16):
        direct(k).start()
    cross(0).start()
    for k in range(1, 16):
        direct(k).wait_recv()
        cross(k).start()
    for k in range(16):
        cross(k).wait()
    for k in range(1, 16):
        direct(k).wait_send()
    own.wait()


def dispatch(slab):
    return pl.pallas_call(
        dispatch_kernel,
        out_shape=jax.ShapeDtypeStruct((16, SLAB, 2 * slab.shape[2]), BF),
        in_specs=[VM],
        out_specs=VM,
        scratch_shapes=[pltpu.SemaphoreType.DMA] + [pltpu.SemaphoreType.DMA((16,))] * 4,
        compiler_params=params(3),
    )(slab)


def combine_kernel(slab_ref, out_ref, got, total, send, recv, ysend, yrecv):
    dp, mp = lax.axis_index("dp"), lax.axis_index("mp")
    half = out_ref.shape[2]
    greet([((dp + k) % 16, mp) for k in range(1, 16)] + [(dp, 1 - mp)])

    def cols(m):
        return pl.ds(pl.multiple_of(m * half, half), half)

    def cross(k):
        s = (dp + k) % 16
        return remote(
            slab_ref.at[s, :, cols(1 - mp)], got.at[s], ysend.at[k], yrecv.at[k], (dp, 1 - mp)
        )

    def direct(k):
        to = (dp + k) % 16
        return remote(total.at[to], out_ref.at[dp], send.at[k], recv.at[k], (to, mp))

    order = list(range(1, 16)) + [0]
    for k in order:
        cross(k).start()
    for k in order:
        s = (dp + k) % 16
        cross(k).wait_recv()
        summed = (slab_ref[s, :, cols(mp)].astype(F32) + got[s].astype(F32)).astype(BF)
        if k == 0:
            out_ref[s] = summed
        else:
            total[s] = summed
            direct(k).start()
    for k in range(16):
        cross(k).wait_send()
    for k in range(1, 16):
        direct(k).wait()


def combine(slab):
    shape = (16, SLAB, slab.shape[2] // 2)
    return pl.pallas_call(
        combine_kernel,
        out_shape=jax.ShapeDtypeStruct(shape, BF),
        in_specs=[VM],
        out_specs=VM,
        scratch_shapes=[pltpu.VMEM(shape, BF), pltpu.VMEM(shape, BF)]
        + [pltpu.SemaphoreType.DMA((16,))] * 4,
        compiler_params=params(4),
    )(slab)


def swap_kernel(back_ref, layer_ref, gate_ref, back_out, layer_out, gate_out, own, send, recv):
    dp, mp = lax.axis_index("dp"), lax.axis_index("mp")
    half = back_ref.shape[1]
    rows = layer_out.shape[0]
    greet([(dp, 1 - mp)])
    mine = pl.ds(pl.multiple_of(mp * half, half), half)

    def part(m):
        return layer_ref.at[pl.ds(pl.multiple_of(m * rows, rows), rows), :]

    copies = [
        remote(gate_ref, gate_out, send.at[0], recv.at[0], (dp, 1 - mp)),
        remote(back_ref, back_out.at[:, mine], send.at[1], recv.at[1], (dp, 1 - mp)),
        remote(part(1 - mp), layer_out.at[:, mine], send.at[2], recv.at[2], (dp, 1 - mp)),
        pltpu.make_async_copy(back_ref, back_out.at[:, mine], own.at[0]),
        pltpu.make_async_copy(part(mp), layer_out.at[:, mine], own.at[1]),
    ]
    for c in copies:
        c.start()
    for c in copies:
        c.wait()


def swap(back, layer, gate):
    length, half = back.shape
    return pl.pallas_call(
        swap_kernel,
        out_shape=(
            jax.ShapeDtypeStruct((length, 2 * half), BF),
            jax.ShapeDtypeStruct((length // 2, 2 * half), BF),
            jax.ShapeDtypeStruct(gate.shape, F32),
        ),
        in_specs=[VM] * 3,
        out_specs=[VM] * 3,
        scratch_shapes=[
            pltpu.SemaphoreType.DMA((2,)),
            pltpu.SemaphoreType.DMA((3,)),
            pltpu.SemaphoreType.DMA((3,)),
        ],
        compiler_params=params(5),
    )(back, layer, gate)


def reduce_kernel(gw_ref, ga_ref, sum_ref, ga_out, sib_got, x_got, up_got, down_got, acc, ga_got, sib_send, sib_recv, x_send, x_recv, z_send, z_recv, ga_send, ga_recv):
    dp, mp, z, x, core = place()
    sib = dp + 1 - 2 * core
    across = dp + 2 - 4 * x
    barrier = pltpu.get_barrier_semaphore()
    for other in ((sib, mp), (across, mp), (dp, 1 - mp)):
        pl.semaphore_signal(barrier, inc=1, device_id=other, device_id_type=MESH)

    @pl.when(z > 0)
    def _():
        pl.semaphore_signal(barrier, inc=1, device_id=(dp - 4, mp), device_id_type=MESH)

    @pl.when(z < 3)
    def _():
        pl.semaphore_signal(barrier, inc=1, device_id=(dp + 4, mp), device_id_type=MESH)

    pl.semaphore_wait(barrier, 3 + jnp.minimum(z, 1) + jnp.minimum(3 - z, 1))

    def rows(b):
        return pl.ds(pl.multiple_of(b * 48, 48), 48)

    def to_sib(xx, zz):
        b = zz * 4 + xx * 2 + 1 - core
        j = xx * 4 + zz
        return remote(
            gw_ref.at[:, rows(b), :], sib_got.at[j], sib_send.at[j], sib_recv.at[j], (sib, mp)
        )

    def to_across(zz):
        return remote(acc.at[0, zz], x_got.at[zz], x_send.at[zz], x_recv.at[zz], (across, mp))

    def to_up(zz):
        return remote(acc.at[1, zz], up_got.at[zz], z_send.at[0, zz], z_recv.at[0, zz], (dp + 4, mp))

    def to_down(zz):
        return remote(
            acc.at[1, zz], down_got.at[zz], z_send.at[1, zz], z_recv.at[1, zz], (dp - 4, mp)
        )

    half = ga_out.shape[0]
    pair = remote(
        ga_ref.at[pl.ds(pl.multiple_of((1 - mp) * half, half), half), :],
        ga_got,
        ga_send,
        ga_recv,
        (dp, 1 - mp),
    )
    order = (0, 3, 1, 2)
    for zz in order:
        to_sib(1 - x, zz).start()
    for zz in order:
        to_sib(x, zz).start()
    pair.start()

    def own(b):
        return gw_ref[:, rows(b), :].astype(F32)

    for zz in order:
        to_sib(1 - x, zz).wait_recv()
        b = zz * 4 + (1 - x) * 2 + core
        acc[0, zz] = (own(b) + sib_got[(1 - x) * 4 + zz].astype(F32)).astype(BF)
        to_across(zz).start()
    for zz in order:
        to_sib(x, zz).wait_recv()
    for zz in order:
        to_across(zz).wait_recv()
        b = zz * 4 + x * 2 + core
        part = own(b) + sib_got[x * 4 + zz].astype(F32) + x_got[zz].astype(F32)
        acc[1, zz] = part.astype(BF)

        @pl.when(jnp.logical_and(zz > z, z > 0))
        def _():
            to_up(zz).wait_recv()
            acc[1, zz] = (acc[1, zz].astype(F32) + up_got[zz].astype(F32)).astype(BF)

        @pl.when(jnp.logical_and(zz < z, z < 3))
        def _():
            to_down(zz).wait_recv()
            acc[1, zz] = (acc[1, zz].astype(F32) + down_got[zz].astype(F32)).astype(BF)

        @pl.when(zz > z)
        def _():
            to_up(zz).start()

        @pl.when(zz < z)
        def _():
            to_down(zz).start()

        @pl.when(zz == z)
        def _():
            sum_ref[...] = part

    @pl.when(z > 0)
    def _():
        to_up(z).wait_recv()
        sum_ref[...] += up_got[z].astype(F32)

    @pl.when(z < 3)
    def _():
        to_down(z).wait_recv()
        sum_ref[...] += down_got[z].astype(F32)

    pair.wait()
    ga_out[...] = (
        ga_ref[pl.ds(pl.multiple_of(mp * half, half), half), :].astype(F32)
        + ga_got[...].astype(F32)
    )
    for zz in range(4):
        to_sib(0, zz).wait_send()
        to_sib(1, zz).wait_send()
        to_across(zz).wait_send()

        @pl.when(zz > z)
        def _():
            to_up(zz).wait_send()

        @pl.when(zz < z)
        def _():
            to_down(zz).wait_send()


def reduce_weights(gw, ga):
    kinds, _, width = gw.shape
    block = (kinds, 48, width)
    half = (ga.shape[0] // 2, ga.shape[1])
    dma = pltpu.SemaphoreType.DMA
    return pl.pallas_call(
        reduce_kernel,
        out_shape=(jax.ShapeDtypeStruct(block, F32), jax.ShapeDtypeStruct(half, F32)),
        in_specs=[VM] * 2,
        out_specs=[VM] * 2,
        scratch_shapes=[
            pltpu.VMEM((8,) + block, BF),
            pltpu.VMEM((4,) + block, BF),
            pltpu.VMEM((4,) + block, BF),
            pltpu.VMEM((4,) + block, BF),
            pltpu.VMEM((2, 4) + block, BF),
            pltpu.VMEM(half, BF),
            dma((8,)),
            dma((8,)),
            dma((4,)),
            dma((4,)),
            dma((2, 4)),
            dma((2, 4)),
            dma,
            dma,
        ],
        compiler_params=params(6),
    )(gw, ga)


def total_kernel(a_ref, o_ref, got, part, send, recv, send2, recv2):
    dp, mp = lax.axis_index("dp"), lax.axis_index("mp")
    me = dp * 2 + mp

    def device(k):
        to = (me + k) % 32
        return (to // 2, to % 2)

    greet([device(k) for k in range(1, 32)])

    def first(k):
        return remote(a_ref.at[(me + k) % 32], got.at[k], send.at[k], recv.at[k], device(k))

    def second(k):
        return remote(part, o_ref.at[me], send2.at[k], recv2.at[k], device(k))

    for k in range(1, 32):
        first(k).start()
    for k in range(1, 32):
        first(k).wait_recv()
    total = a_ref[me]
    for k in range(1, 32):
        total = total + got[k]
    part[...] = total
    o_ref[me] = total
    for k in range(1, 32):
        second(k).start()
    for k in range(1, 32):
        second(k).wait()
    for k in range(1, 32):
        first(k).wait_send()


def total_everywhere(arrays):
    sizes = [a.size for a in arrays]
    flat = jnp.concatenate([a.reshape(-1) for a in arrays])
    packed = jnp.pad(flat, (0, 32 * 8 * 128 - flat.size)).reshape(32, 8, 128)
    dma = pltpu.SemaphoreType.DMA
    out = pl.pallas_call(
        total_kernel,
        out_shape=jax.ShapeDtypeStruct(packed.shape, F32),
        in_specs=[VM],
        out_specs=VM,
        scratch_shapes=[pltpu.VMEM(packed.shape, F32), pltpu.VMEM((8, 128), F32)]
        + [dma((32,))] * 4,
        compiler_params=params(7),
    )(packed).reshape(-1)
    ends, at = [], 0
    for s in sizes:
        ends.append(out[at : at + s])
        at += s
    return [e.reshape(a.shape) for e, a in zip(ends, arrays)]


def local_pairs(
    tokens,
    w_query,
    w_key,
    w_value,
    w_output,
    bias_table,
    gain_attn,
    gain_moe,
    router,
    w_in,
    w_out,
    routes,
    slots,
    buckets,
    cotangent,
):
    length, width = tokens.shape
    half_rows, half = length // 2, width // 2
    mp_rank = lax.axis_index("mp")
    experts = router.shape[1]
    capacity = (5 * length + 4 * experts - 1) // (4 * experts)
    head_width = w_query.shape[1]
    heads = head_width // HEAD_DIM

    def own_rows(array):
        return lax.dynamic_slice_in_dim(array, mp_rank * half_rows, half_rows, 0)

    def own_cols(array):
        return lax.dynamic_slice_in_dim(array, mp_rank * half, half, 1)

    weights = gather_weights(jnp.stack([w_query, w_key, w_value, w_output.T]))
    bucket_hot = (
        buckets[:, None] == jnp.arange(bias_table.shape[0], dtype=jnp.int32)[None, :]
    ).astype(F32)
    bucket_hot = jnp.pad(bucket_hot, ((0, 1), (0, 0)))
    table_heads = lax.dynamic_slice_in_dim(bias_table, mp_rank * heads, heads, 1)
    table_heads = jnp.pad(table_heads, ((0, 0), (0, 8 - heads)))
    offsets = jnp.einsum("ob,bh->ho", bucket_hot, table_heads, precision=lax.Precision.HIGHEST)
    partial, normed_attn, qkv, context, chances = pl.pallas_call(
        lambda *refs: forward_kernel(heads, *refs),
        out_shape=(
            jax.ShapeDtypeStruct((length, width), BF),
            jax.ShapeDtypeStruct((length, width), BF),
            jax.ShapeDtypeStruct((3, length, head_width), BF),
            jax.ShapeDtypeStruct((length, head_width), BF),
            jax.ShapeDtypeStruct((heads, length, length), F32),
        ),
        in_specs=[VM] * 4,
        out_specs=[VM] * 5,
        compiler_params=params(),
    )(tokens, gain_attn[None, :], weights, offsets)
    inputs = tokens.astype(F32)
    residual = inputs + pair_sum(partial)
    moe_float, inverse_moe = normalize(residual, gain_moe)
    normed_moe = moe_float.astype(BF)
    logits = jnp.dot(normed_moe, router, preferred_element_type=F32)
    chance_all = jax.nn.softmax(logits, axis=-1)
    route_hot = (routes[:, None] == jnp.arange(experts, dtype=jnp.int32)[None, :]).astype(F32)
    gates = jnp.sum(chance_all * route_hot, axis=1)
    gradient = cotangent.astype(F32)
    grad_rows = (gates[:, None] * gradient).astype(BF)
    spots = jnp.arange(experts * SLAB, dtype=jnp.int32)[:, None]
    target = (routes * SLAB + slots)[None, :]
    hot_in = (spots == target).astype(BF)
    hot_grad = (spots == target + capacity).astype(BF)
    slab = jnp.dot(
        jnp.concatenate([hot_in, hot_grad], axis=1),
        jnp.concatenate([own_cols(normed_moe), own_cols(grad_rows)], axis=0),
        preferred_element_type=F32,
    ).astype(BF)
    arrived = dispatch(slab.reshape(experts, SLAB, half))
    expert_input = arrived[:, :capacity].reshape(-1, width)
    grad_expert = arrived[:, capacity : 2 * capacity].reshape(-1, width)
    hidden_pre = jnp.dot(expert_input, w_in[0], preferred_element_type=F32)
    gelu_value, gelu_back = jax.vjp(lambda inner: jax.nn.gelu(inner, approximate=False), hidden_pre)
    hidden = gelu_value.astype(BF)
    partial_out = jnp.dot(hidden, w_out[0], preferred_element_type=F32).astype(BF)
    grad_hidden = jnp.einsum("rd,fd->rf", grad_expert, w_out[0], preferred_element_type=F32)
    grad_pre = gelu_back(grad_hidden)[0].astype(BF)
    partial_back = jnp.einsum("rf,df->rd", grad_pre, w_in[0], preferred_element_type=F32).astype(BF)
    grad_w_out = jnp.einsum("rf,rd->fd", hidden, grad_expert, preferred_element_type=F32)[None]
    grad_w_in = jnp.einsum("rd,rf->df", expert_input, grad_pre, preferred_element_type=F32)[None]
    back_slab = jnp.concatenate(
        [
            partial_out.reshape(experts, capacity, width),
            partial_back.reshape(experts, capacity, width),
            jnp.zeros((experts, SLAB - 2 * capacity, width), BF),
        ],
        axis=1,
    )
    returned = combine(back_slab).reshape(experts * SLAB, half)
    expert_rows = dot(hot_in, returned, (0, 0))
    back_half = dot(hot_grad, returned, (0, 0)).astype(BF)
    layer_half = (own_cols(residual) + gates[:, None] * expert_rows).astype(BF)
    gate_half = jnp.sum(own_cols(gradient) * expert_rows, axis=1)
    grad_slots, layer_out, gate_other = swap(
        back_half, layer_half, jnp.broadcast_to(gate_half[None, :], (8, length))
    )
    grad_gates = gate_half + gate_other[0]
    grad_logits = (grad_gates[:, None] * gates[:, None] * (route_hot - chance_all)).astype(BF)
    grad_normed = grad_slots.astype(F32) + jnp.einsum(
        "se,de->sd", grad_logits, router, preferred_element_type=F32
    )
    grad_residual = gradient + norm_backward(residual, inverse_moe, gain_moe, grad_normed)
    grad_gain_moe = jnp.sum(own_rows(grad_normed) * own_rows(residual * inverse_moe), axis=0)
    grad_router = jnp.einsum(
        "sd,se->de", own_rows(normed_moe), own_rows(grad_logits), preferred_element_type=F32
    )
    grad_weights, grad_attn, grad_offsets = pl.pallas_call(
        lambda *refs: backward_kernel(heads, *refs),
        out_shape=(
            jax.ShapeDtypeStruct(weights.shape, BF),
            jax.ShapeDtypeStruct((length, width), BF),
            jax.ShapeDtypeStruct((8, 2 * length), F32),
        ),
        in_specs=[VM] * 6,
        out_specs=[VM] * 3,
        scratch_shapes=[
            pltpu.VMEM((length, head_width), BF),
            pltpu.VMEM((3, length, head_width), BF),
        ],
        compiler_params=params(),
    )(grad_residual.astype(BF), normed_attn, weights, qkv, context, chances)
    sums, own_grad_attn = reduce_weights(grad_weights, grad_attn)
    own_inputs = own_rows(inputs)
    own_inverse = lax.rsqrt(jnp.mean(own_inputs * own_inputs, axis=-1, keepdims=True) + EPS)
    input_grad = own_rows(grad_residual) + norm_backward(
        own_inputs, own_inverse, gain_attn, own_grad_attn
    )
    grad_gain_attn = jnp.sum(own_grad_attn * own_inputs * own_inverse, axis=0)
    table_part = jnp.einsum(
        "ob,ho->bh", bucket_hot, grad_offsets, precision=lax.Precision.HIGHEST
    )[:, :heads]
    table_full = lax.dynamic_update_slice_in_dim(
        jnp.zeros(bias_table.shape, F32), table_part, mp_rank * heads, 1
    )
    grad_table, gain_attn_total, gain_moe_total, router_total = total_everywhere(
        [table_full, grad_gain_attn, grad_gain_moe, grad_router]
    )
    return (
        layer_out,
        input_grad,
        sums[0],
        sums[1],
        sums[2],
        sums[3].T,
        grad_table,
        gain_attn_total,
        gain_moe_total,
        router_total,
        grad_w_in,
        grad_w_out,
    )


def solution(mesh):
    in_specs = (
        P("dp", None),
        P("dp", "mp"),
        P("dp", "mp"),
        P("dp", "mp"),
        P("mp", "dp"),
        P(),
        P(),
        P(),
        P(),
        P("dp", None, "mp"),
        P("dp", "mp", None),
        P("dp"),
        P("dp"),
        P(),
        P("dp", None),
    )
    out_specs = (
        P(("dp", "mp"), None),
        P(("dp", "mp"), None),
        P("dp", "mp"),
        P("dp", "mp"),
        P("dp", "mp"),
        P("mp", "dp"),
        P(),
        P(),
        P(),
        P(),
        P("dp", None, "mp"),
        P("dp", "mp", None),
    )
    small = mesh.shape["mp"] == 2 and mesh.shape["dp"] == 16
    return jax.shard_map(local_pairs if small else local, mesh=mesh, in_specs=in_specs, out_specs=out_specs, check_vma=False)
```

```python
import jax
import jax.numpy as jnp
from jax import lax
from jax.experimental import pallas as pl
from jax.experimental.pallas import tpu as pltpu
from jax.sharding import PartitionSpec as P

HEAD_DIM = 64


EPS = 1e-06
query_rows = 512


def in_blocks(array, dim, count):
    lengths = array.shape
    tiles = array.reshape(*lengths[:dim], count, lengths[dim] // count, *lengths[dim + 1 :])
    return jnp.moveaxis(tiles, dim, 0)


def sum_at_owner(array, axis, dim):
    count = lax.axis_size(axis)
    tiles = lax.all_to_all(in_blocks(array, dim, count), axis, 0, 0, tiled=True)
    return jnp.sum(tiles.astype(jnp.float32), axis=0)


def in_one_piece(arrays, axis, dim, along):
    ends, at = ([], 0)
    for a in arrays[:-1]:
        at += a.shape[along]
        ends.append(at)
    both = jnp.concatenate(arrays, axis=along)
    return tuple(jnp.split(sum_at_owner(both, axis, dim), ends, axis=along))


def normalize(inputs, gains):
    inverse = lax.rsqrt(jnp.mean(inputs * inputs, axis=-1, keepdims=True) + EPS)
    return (inputs * inverse * gains, inverse)


def norm_backward(inputs, inverse, gains, gradient):
    unit_rows = inputs * inverse
    scaled = gradient * gains
    return inverse * (scaled - unit_rows * jnp.mean(unit_rows * scaled, axis=-1, keepdims=True))


def offset_band(offset_bias, row_count, key_count):
    head_count = offset_bias.shape[0]
    window = offset_bias
    window = jnp.concatenate([window, jnp.zeros((head_count, 1), window.dtype)], axis=1)
    turned = jnp.concatenate([window[:, row_count - 1 :], window[:, : row_count - 1]], axis=1)
    span = row_count + key_count - 1
    repeated = jnp.tile(turned, (1, row_count))[:, : row_count * span]
    return repeated.reshape(head_count, row_count, span)[:, :, :key_count]


def band_sums(gradient, row_count, key_count):
    head_count = gradient.shape[0]
    padded = jnp.concatenate(
        [jnp.zeros((head_count, row_count, row_count), gradient.dtype), gradient], axis=2
    )
    flattened = jnp.concatenate(
        [padded.reshape(head_count, -1), jnp.zeros((head_count, row_count), gradient.dtype)], axis=1
    )
    skewed = flattened.reshape(head_count, row_count, row_count + key_count + 1)
    return jnp.sum(skewed, axis=1)[:, 1 : row_count + key_count]


def local(
    tokens,
    w_query,
    w_key,
    w_value,
    w_output,
    bias_table,
    gain_attn,
    gain_moe,
    router,
    w_in,
    w_out,
    routes,
    slots,
    buckets,
    cotangent,
):
    length, model_width = tokens.shape
    mp_count = lax.axis_size("mp")
    mp_rank = lax.axis_index("mp")
    own_rows = length // mp_count
    own_first = mp_rank * own_rows
    experts = router.shape[1]
    capacity = (5 * length + 4 * experts - 1) // (4 * experts)
    head_width = w_query.shape[1]
    head_count = head_width // HEAD_DIM
    row_block = min(query_rows, length)
    block_count = length // row_block
    block_starts = jnp.arange(block_count, dtype=jnp.int32) * row_block

    def own_slice(array):
        return lax.dynamic_slice_in_dim(array, own_first, own_rows, 0)

    inputs = tokens.astype(jnp.float32)
    normed_float, inverse_attn = normalize(inputs, gain_attn)
    normed_attn = normed_float.astype(jnp.bfloat16)
    full_query, full_key, full_value, full_output = (
        lax.all_gather(w_query, "dp", axis=0, tiled=True),
        lax.all_gather(w_key, "dp", axis=0, tiled=True),
        lax.all_gather(w_value, "dp", axis=0, tiled=True),
        lax.all_gather(w_output, "dp", axis=1, tiled=True),
    )
    w_joint = jnp.concatenate([full_query, full_key, full_value], axis=1)
    projected = jnp.dot(normed_attn, w_joint, preferred_element_type=jnp.float32).astype(
        jnp.bfloat16
    )
    queries = projected[:, :head_width].reshape(length, head_count, HEAD_DIM)
    keys_all = projected[:, head_width : 2 * head_width].reshape(length, head_count, HEAD_DIM)
    values = projected[:, 2 * head_width :].reshape(length, head_count, HEAD_DIM)
    bucket_hot = (
        buckets[:, None] == jnp.arange(bias_table.shape[0], dtype=jnp.int32)[None, :]
    ).astype(jnp.float32)
    table_heads = lax.dynamic_slice_in_dim(bias_table, mp_rank * head_count, head_count, 1)
    offset_bias = jnp.einsum("ob,bh->ho", bucket_hot, table_heads, precision=lax.Precision.HIGHEST)

    def attend_block(first_row):
        scores = jnp.einsum(
            "qhd,khd->hqk", queries, keys_all, preferred_element_type=jnp.float32
        ) + offset_band(offset_bias, row_block, length)
        peak_score = jnp.max(scores, axis=-1, keepdims=True)
        weights = jnp.exp(scores - peak_score)
        summed = jnp.sum(weights, axis=-1, keepdims=True)
        chances = (weights / summed).astype(jnp.bfloat16)
        context_rows = jnp.einsum(
            "hqk,khd->qhd", chances, values, preferred_element_type=jnp.float32
        )
        return (context_rows.astype(jnp.bfloat16), (peak_score + jnp.log(summed))[:, :, 0])

    context_blocks, log_totals = lax.map(attend_block, block_starts)
    context = context_blocks.reshape(length, head_width)
    partial_attn = jnp.dot(context, full_output, preferred_element_type=jnp.float32)
    attended = lax.psum(partial_attn.astype(jnp.bfloat16), "mp").astype(jnp.float32)
    residual = inputs + attended
    moe_float, inverse_moe = normalize(residual, gain_moe)
    normed_moe = moe_float.astype(jnp.bfloat16)
    logits = jnp.dot(normed_moe, router, preferred_element_type=jnp.float32)
    chance_all = jax.nn.softmax(logits, axis=-1)
    route_hot = (routes[:, None] == jnp.arange(experts, dtype=jnp.int32)[None, :]).astype(
        jnp.float32
    )
    gates = jnp.sum(chance_all * route_hot, axis=1)
    target = routes * capacity + slots
    slotted = (
        jnp.zeros((experts * capacity, model_width), jnp.bfloat16)
        .at[target]
        .set(normed_moe)
        .reshape(experts, capacity, model_width)
    )
    arrived = lax.all_to_all(slotted, "dp", split_axis=0, concat_axis=0, tiled=True)
    expert_input = arrived.reshape(-1, model_width)
    hidden_pre = jnp.dot(expert_input, w_in[0], preferred_element_type=jnp.float32)
    gelu_value, gelu_back = jax.vjp(lambda inner: jax.nn.gelu(inner, approximate=False), hidden_pre)
    hidden = gelu_value.astype(jnp.bfloat16)
    partial_out = jnp.dot(hidden, w_out[0], preferred_element_type=jnp.float32).reshape(
        arrived.shape
    )
    summed_out = lax.psum(partial_out.astype(jnp.bfloat16), "mp")
    returned = lax.all_to_all(summed_out, "dp", split_axis=0, concat_axis=0, tiled=True)
    expert_rows = returned.reshape(experts * capacity, model_width)[target].astype(jnp.float32)
    layer_full = residual + gates[:, None] * expert_rows
    layer_out = own_slice(layer_full).astype(jnp.bfloat16)
    gradient = cotangent.astype(jnp.float32)
    grad_gates = jnp.sum(gradient * expert_rows, axis=1)
    grad_rows = (gates[:, None] * gradient).astype(jnp.bfloat16)
    grad_slotted = (
        jnp.zeros((experts * capacity, model_width), jnp.bfloat16)
        .at[target]
        .set(grad_rows)
        .reshape(experts, capacity, model_width)
    )
    grad_arrived = lax.all_to_all(grad_slotted, "dp", split_axis=0, concat_axis=0, tiled=True)
    grad_expert = grad_arrived.reshape(-1, model_width)
    grad_hidden = jnp.einsum("rd,fd->rf", grad_expert, w_out[0], preferred_element_type=jnp.float32)
    grad_pre = gelu_back(grad_hidden)[0].astype(jnp.bfloat16)
    grad_w_out = jnp.einsum("rf,rd->fd", hidden, grad_expert, preferred_element_type=jnp.float32)[
        None
    ]
    grad_w_in = jnp.einsum("rd,rf->df", expert_input, grad_pre, preferred_element_type=jnp.float32)[
        None
    ]
    partial_back = jnp.einsum(
        "rf,df->rd", grad_pre, w_in[0], preferred_element_type=jnp.float32
    ).reshape(arrived.shape)
    grad_input_slots = lax.psum(partial_back.astype(jnp.bfloat16), "mp")
    grad_sent = lax.all_to_all(grad_input_slots, "dp", split_axis=0, concat_axis=0, tiled=True)
    grad_normed = grad_sent.reshape(experts * capacity, model_width)[target].astype(jnp.float32)
    grad_logits = (grad_gates[:, None] * gates[:, None] * (route_hot - chance_all)).astype(
        jnp.bfloat16
    )
    grad_normed = grad_normed + jnp.einsum(
        "se,de->sd", grad_logits, router, preferred_element_type=jnp.float32
    )
    grad_residual = gradient + norm_backward(residual, inverse_moe, gain_moe, grad_normed)
    grad_gain_moe = jnp.sum(own_slice(grad_normed) * own_slice(residual * inverse_moe), axis=0)
    grad_router = jnp.einsum(
        "sd,se->de",
        own_slice(normed_moe),
        own_slice(grad_logits),
        preferred_element_type=jnp.float32,
    )
    grad_attended = grad_residual.astype(jnp.bfloat16)
    grad_output = jnp.einsum(
        "sk,sd->kd", context, grad_attended, preferred_element_type=jnp.float32
    )
    grad_context = (
        jnp.einsum("sd,kd->sk", grad_attended, full_output, preferred_element_type=jnp.float32)
        .astype(jnp.bfloat16)
        .reshape(length, head_count, HEAD_DIM)
    )

    def back_block(running, items):
        first_row, log_total = items
        grad_keys, grad_values, grad_offsets = running
        scores = jnp.einsum(
            "qhd,khd->hqk", queries, keys_all, preferred_element_type=jnp.float32
        ) + offset_band(offset_bias, row_block, length)
        chances = jnp.exp(scores - log_total[:, :, None])
        grad_chances = jnp.einsum(
            "qhd,khd->hqk", grad_context, values, preferred_element_type=jnp.float32
        )
        grad_scores = chances * (
            grad_chances - jnp.sum(grad_chances * chances, axis=-1, keepdims=True)
        )
        grad_offsets = grad_offsets + band_sums(grad_scores, row_block, length)
        grad_low = grad_scores.astype(jnp.bfloat16)
        grad_queries = jnp.einsum(
            "hqk,khd->qhd", grad_low, keys_all, preferred_element_type=jnp.float32
        )
        grad_keys = grad_keys + jnp.einsum(
            "hqk,qhd->khd", grad_low, queries, preferred_element_type=jnp.float32
        )
        grad_values = grad_values + jnp.einsum(
            "hqk,qhd->khd",
            chances.astype(jnp.bfloat16),
            grad_context,
            preferred_element_type=jnp.float32,
        )
        return ((grad_keys, grad_values, grad_offsets), grad_queries.astype(jnp.bfloat16))

    zero_heads = jnp.zeros((length, head_count, HEAD_DIM), jnp.float32)
    zero_offsets = jnp.zeros((head_count, 2 * length - 1), jnp.float32)
    (grad_keys, grad_values, grad_offsets), grad_queries = lax.scan(
        back_block, (zero_heads, zero_heads, zero_offsets), (block_starts, log_totals)
    )
    grad_joint = jnp.concatenate(
        [
            grad_queries.reshape(length, head_width),
            grad_keys.astype(jnp.bfloat16).reshape(length, head_width),
            grad_values.astype(jnp.bfloat16).reshape(length, head_width),
        ],
        axis=1,
    )
    grad_weights = jnp.einsum(
        "sd,sk->dk", normed_attn, grad_joint, preferred_element_type=jnp.float32
    )
    grad_query, grad_key, grad_value, grad_out_proj = (
        *in_one_piece(
            (
                grad_weights[:, :head_width].astype(jnp.bfloat16),
                grad_weights[:, head_width : 2 * head_width].astype(jnp.bfloat16),
                grad_weights[:, 2 * head_width :].astype(jnp.bfloat16),
            ),
            "dp",
            0,
            1,
        ),
        sum_at_owner(grad_output.astype(jnp.bfloat16), "dp", 1),
    )
    own_grad_attn = lax.psum_scatter(
        jnp.einsum("sk,dk->sd", grad_joint, w_joint, preferred_element_type=jnp.float32).astype(
            jnp.bfloat16
        ),
        "mp",
        scatter_dimension=0,
        tiled=True,
    ).astype(jnp.float32)
    own_inputs = own_slice(inputs)
    own_inverse = own_slice(inverse_attn)
    input_grad = own_slice(grad_residual) + norm_backward(
        own_inputs, own_inverse, gain_attn, own_grad_attn
    )
    grad_gain_attn = jnp.sum(own_grad_attn * own_inputs * own_inverse, axis=0)
    table_part = jnp.einsum("ob,ho->bh", bucket_hot, grad_offsets, precision=lax.Precision.HIGHEST)
    table_full = lax.dynamic_update_slice_in_dim(
        jnp.zeros(bias_table.shape, jnp.float32), table_part, mp_rank * head_count, 1
    )
    grad_table, gain_attn_total, gain_moe_total, router_total = lax.psum(
        (table_full, grad_gain_attn, grad_gain_moe, grad_router), ("dp", "mp")
    )
    return (
        layer_out,
        input_grad,
        grad_query,
        grad_key,
        grad_value,
        grad_out_proj,
        grad_table,
        gain_attn_total,
        gain_moe_total,
        router_total,
        grad_w_in,
        grad_w_out,
    )


BF = jnp.bfloat16
F32 = jnp.float32
MESH = pl.DeviceIdType.MESH
VM = pl.BlockSpec(memory_space=pltpu.VMEM)
SLAB = 48


def params(collective_id=None):
    if collective_id is None:
        return pltpu.CompilerParams(vmem_limit_bytes=48 * 2**20)
    return pltpu.CompilerParams(
        vmem_limit_bytes=48 * 2**20, collective_id=collective_id, has_side_effects=True
    )


def dot(a, b, dims):
    return lax.dot_general(a, b, ((dims[:1], dims[1:]), ((), ())), preferred_element_type=F32)


def greet(devices):
    barrier = pltpu.get_barrier_semaphore()
    for device in devices:
        pl.semaphore_signal(barrier, inc=1, device_id=device, device_id_type=MESH)
    pl.semaphore_wait(barrier, len(devices))


def remote(src, dst, send, recv, device):
    return pltpu.make_async_remote_copy(
        src_ref=src, dst_ref=dst, send_sem=send, recv_sem=recv, device_id=device, device_id_type=MESH
    )


def place():
    dp = lax.axis_index("dp")
    return dp, lax.axis_index("mp"), dp // 4, (dp // 2) % 2, dp % 2


def gather_kernel(own_ref, out_ref, own_sem, send, recv):
    dp, mp, z, x, core = place()
    sib = dp + 1 - 2 * core
    across = dp + 2 - 4 * x
    barrier = pltpu.get_barrier_semaphore()
    for other in (sib, across):
        pl.semaphore_signal(barrier, inc=1, device_id=(other, mp), device_id_type=MESH)

    @pl.when(z > 0)
    def _():
        pl.semaphore_signal(barrier, inc=1, device_id=(dp - 4, mp), device_id_type=MESH)

    @pl.when(z < 3)
    def _():
        pl.semaphore_signal(barrier, inc=1, device_id=(dp + 4, mp), device_id_type=MESH)

    pl.semaphore_wait(barrier, 2 + jnp.minimum(z, 1) + jnp.minimum(3 - z, 1))

    def block(b):
        return out_ref.at[:, pl.ds(pl.multiple_of(b * 48, 48), 48), :]

    def copy(b, way, device, src=None):
        return remote(
            block(b) if src is None else src, block(b), send.at[way, b], recv.at[b], (device, mp)
        )

    own = pltpu.make_async_copy(own_ref, block(dp), own_sem)
    own.start()

    def spread(b, src, up, down):
        @pl.when(jnp.logical_and(up, z < 3))
        def _():
            copy(b, 0, dp + 4, src).start()

        @pl.when(jnp.logical_and(down, z > 0))
        def _():
            copy(b, 1, dp - 4, src).start()

        copy(b, 2, across, src).start()
        copy(b, 3, sib, src).start()

    spread(dp, own_ref, True, True)
    for s in (1, 2, 3):

        @pl.when(z - s >= 0)
        def _():
            b = dp - 4 * s
            copy(b, 0, sib).wait_recv()
            spread(b, None, True, False)

        @pl.when(z + s <= 3)
        def _():
            b = dp + 4 * s
            copy(b, 0, sib).wait_recv()
            spread(b, None, False, True)

    for s in range(4):
        for sign in (1, -1) if s else (1,):

            @pl.when(jnp.logical_and(z + sign * s >= 0, z + sign * s <= 3))
            def _():
                b = across + 4 * s * sign
                copy(b, 0, sib).wait_recv()
                copy(b, 3, sib).start()

    for zz in range(4):
        for xx in range(2):
            copy(zz * 4 + xx * 2 + 1 - core, 3, sib).wait_recv()
    own.wait()
    for zz in range(4):
        b = zz * 4 + x * 2 + core

        @pl.when(jnp.logical_and(zz <= z, z < 3))
        def _():
            copy(b, 0, sib).wait_send()

        @pl.when(jnp.logical_and(zz >= z, z > 0))
        def _():
            copy(b, 1, sib).wait_send()

        copy(b, 2, sib).wait_send()
        copy(b, 3, sib).wait_send()
        copy(zz * 4 + (1 - x) * 2 + core, 3, sib).wait_send()


def gather_weights(own):
    return pl.pallas_call(
        gather_kernel,
        out_shape=jax.ShapeDtypeStruct((own.shape[0], 768, own.shape[2]), BF),
        in_specs=[VM],
        out_specs=VM,
        scratch_shapes=[
            pltpu.SemaphoreType.DMA,
            pltpu.SemaphoreType.DMA((4, 16)),
            pltpu.SemaphoreType.DMA((16,)),
        ],
        compiler_params=params(1),
    )(own)


def forward_kernel(heads, tokens_ref, gain_ref, w_ref, off_ref, part_ref, normed_ref, qkv_ref, ctx_ref, p_ref):
    x = tokens_ref[...].astype(F32)
    normed = normalize(x, gain_ref[...])[0].astype(BF)
    normed_ref[...] = normed
    for j in range(3):
        qkv_ref[j] = dot(normed, w_ref[j], (1, 0)).astype(BF)
    length = x.shape[0]
    for h in range(heads):
        cols = slice(h * HEAD_DIM, (h + 1) * HEAD_DIM)
        row = jnp.broadcast_to(off_ref[h : h + 1, :], (length, 2 * length))
        bias = pltpu.roll(row, length + 1, 1, stride=1, stride_axis=0)[:, :length]
        scores = dot(qkv_ref[0, :, cols], qkv_ref[1, :, cols], (1, 1)) + bias
        weights = jnp.exp(scores - jnp.max(scores, axis=-1, keepdims=True))
        chances = weights / jnp.sum(weights, axis=-1, keepdims=True)
        p_ref[h] = chances
        ctx_ref[:, cols] = dot(chances.astype(BF), qkv_ref[2, :, cols], (1, 0)).astype(BF)
    part_ref[...] = dot(ctx_ref[...], w_ref[3], (1, 1)).astype(BF)


def backward_kernel(heads, g_ref, normed_ref, w_ref, qkv_ref, ctx_ref, p_ref, gw_ref, ga_ref, goff_ref, gc_ref, gj_ref):
    length = g_ref.shape[0]
    grad = g_ref[...]
    gw_ref[3] = dot(grad, ctx_ref[...], (0, 0)).astype(BF)
    gc_ref[...] = dot(grad, w_ref[3], (1, 0)).astype(BF)
    flip = (
        lax.broadcasted_iota(jnp.int32, (length, length), 0)
        + lax.broadcasted_iota(jnp.int32, (length, length), 1)
        == length - 1
    ).astype(F32).astype(BF)
    zeros = jnp.zeros((length, length), F32)
    goff_ref[...] = jnp.zeros_like(goff_ref)
    for h in range(heads):
        cols = slice(h * HEAD_DIM, (h + 1) * HEAD_DIM)
        chances = p_ref[h]
        gctx = gc_ref[:, cols]
        grad_chances = dot(gctx, qkv_ref[2, :, cols], (1, 1))
        grad_scores = chances * (
            grad_chances - jnp.sum(grad_chances * chances, axis=-1, keepdims=True)
        )
        high = grad_scores.astype(BF)
        rest = (grad_scores - high.astype(F32)).astype(BF)
        flipped = dot(flip, high, (1, 0)) + dot(flip, rest, (1, 0))
        skewed = pltpu.roll(
            jnp.concatenate([flipped, zeros], axis=1), 0, 1, stride=1, stride_axis=0
        )
        goff_ref[h : h + 1, :] = jnp.sum(skewed, axis=0, keepdims=True)
        gj_ref[0, :, cols] = dot(high, qkv_ref[1, :, cols], (1, 0)).astype(BF)
        gj_ref[1, :, cols] = dot(high, qkv_ref[0, :, cols], (0, 0)).astype(BF)
        gj_ref[2, :, cols] = dot(chances.astype(BF), gctx, (0, 0)).astype(BF)
    total = None
    for j in range(3):
        gw_ref[j] = dot(normed_ref[...], gj_ref[j], (0, 0)).astype(BF)
        term = dot(gj_ref[j], w_ref[j], (1, 1))
        total = term if total is None else total + term
    ga_ref[...] = total.astype(BF)


def pair_kernel(a_ref, o_ref, got, send, recv):
    dp, mp = lax.axis_index("dp"), lax.axis_index("mp")
    greet([(dp, 1 - mp)])
    c = remote(a_ref, got, send, recv, (dp, 1 - mp))
    c.start()
    c.wait()
    o_ref[...] = a_ref[...].astype(F32) + got[...].astype(F32)


def pair_sum(a):
    return pl.pallas_call(
        pair_kernel,
        out_shape=jax.ShapeDtypeStruct(a.shape, F32),
        in_specs=[VM],
        out_specs=VM,
        scratch_shapes=[pltpu.VMEM(a.shape, a.dtype), pltpu.SemaphoreType.DMA, pltpu.SemaphoreType.DMA],
        compiler_params=params(2),
    )(a)


def dispatch_kernel(slab_ref, out_ref, own_sem, send, recv, ysend, yrecv):
    dp, mp = lax.axis_index("dp"), lax.axis_index("mp")
    half = slab_ref.shape[2]
    greet([((dp + k) % 16, mp) for k in range(1, 16)] + [(dp, 1 - mp)])

    def spot(s, m):
        return out_ref.at[s, :, pl.ds(pl.multiple_of(m * half, half), half)]

    own = pltpu.make_async_copy(slab_ref.at[dp], spot(dp, mp), own_sem)
    own.start()

    def cross(k):
        s = (dp + 16 - k) % 16
        src = slab_ref.at[dp] if k == 0 else spot(s, mp)
        return remote(src, spot(s, mp), ysend.at[k], yrecv.at[k], (dp, 1 - mp))

    def direct(k):
        to = (dp + k) % 16
        return remote(slab_ref.at[to], spot(dp, mp), send.at[k], recv.at[k], (to, mp))

    for k in range(1, 16):
        direct(k).start()
    cross(0).start()
    for k in range(1, 16):
        direct(k).wait_recv()
        cross(k).start()
    for k in range(16):
        cross(k).wait()
    for k in range(1, 16):
        direct(k).wait_send()
    own.wait()


def dispatch(slab):
    return pl.pallas_call(
        dispatch_kernel,
        out_shape=jax.ShapeDtypeStruct((16, SLAB, 2 * slab.shape[2]), BF),
        in_specs=[VM],
        out_specs=VM,
        scratch_shapes=[pltpu.SemaphoreType.DMA] + [pltpu.SemaphoreType.DMA((16,))] * 4,
        compiler_params=params(3),
    )(slab)


def expert_kernel(capacity, arrived_ref, w_in_ref, w_out_ref, slab_ref, gin_ref, gout_ref, x_ref, g_ref, out_ref, back_ref):
    step, last = pl.program_id(0), pl.num_programs(0) - 1
    packed = x_ref.shape[0]
    count = packed // capacity

    def chooser(first):
        row = lax.broadcasted_iota(jnp.int32, (packed, count * SLAB), 0)
        col = lax.broadcasted_iota(jnp.int32, (packed, count * SLAB), 1)
        return (col == row + row // capacity * (SLAB - capacity) + first).astype(F32).astype(BF)

    @pl.when(step == 0)
    def _():
        x_ref[...] = dot(chooser(0), arrived_ref[...], (1, 0)).astype(BF)
        g_ref[...] = dot(chooser(capacity), arrived_ref[...], (1, 0)).astype(BF)
        out_ref[...] = jnp.zeros_like(out_ref)
        back_ref[...] = jnp.zeros_like(back_ref)

    pre = dot(x_ref[...], w_in_ref[0], (1, 0))
    share = 0.5 * (1.0 + lax.erf(pre * (0.5**0.5)))
    hidden = (pre * share).astype(BF)
    slope = share + pre * jnp.exp(-0.5 * pre * pre) * ((0.5 / jnp.pi) ** 0.5)
    out_ref[...] += dot(hidden, w_out_ref[0], (1, 0))
    grad_pre = (slope * dot(g_ref[...], w_out_ref[0], (1, 1))).astype(BF)
    back_ref[...] += dot(grad_pre, w_in_ref[0], (1, 1))
    gout_ref[0] = dot(hidden, g_ref[...], (0, 0))
    gin_ref[0] = dot(x_ref[...], grad_pre, (0, 0))

    @pl.when(step == last)
    def _():
        slab_ref[...] = (
            dot(chooser(0), out_ref[...].astype(BF), (0, 0))
            + dot(chooser(capacity), back_ref[...].astype(BF), (0, 0))
        ).astype(BF)


def expert_layer(arrived, w_in, w_out, capacity):
    count, _, width = arrived.shape
    inner = w_in.shape[2]
    tile = 256
    packed = count * capacity
    whole = pl.BlockSpec((count * SLAB, width), lambda i: (0, 0))
    in_tile = pl.BlockSpec((1, width, tile), lambda i: (0, 0, i))
    out_tile = pl.BlockSpec((1, tile, width), lambda i: (0, i, 0))
    slab, gin, gout = pl.pallas_call(
        lambda *refs: expert_kernel(capacity, *refs),
        grid=(inner // tile,),
        out_shape=(
            jax.ShapeDtypeStruct((count * SLAB, width), BF),
            jax.ShapeDtypeStruct(w_in.shape, F32),
            jax.ShapeDtypeStruct(w_out.shape, F32),
        ),
        in_specs=[whole, in_tile, out_tile],
        out_specs=(whole, in_tile, out_tile),
        scratch_shapes=[
            pltpu.VMEM((packed, width), BF),
            pltpu.VMEM((packed, width), BF),
            pltpu.VMEM((packed, width), F32),
            pltpu.VMEM((packed, width), F32),
        ],
        compiler_params=params(),
    )(arrived.reshape(count * SLAB, width), w_in, w_out)
    return slab.reshape(arrived.shape), gin, gout


def combine_kernel(slab_ref, out_ref, got, total, send, recv, ysend, yrecv):
    dp, mp = lax.axis_index("dp"), lax.axis_index("mp")
    half = out_ref.shape[2]
    greet([((dp + k) % 16, mp) for k in range(1, 16)] + [(dp, 1 - mp)])

    def cols(m):
        return pl.ds(pl.multiple_of(m * half, half), half)

    def cross(k):
        s = (dp + k) % 16
        return remote(
            slab_ref.at[s, :, cols(1 - mp)], got.at[s], ysend.at[k], yrecv.at[k], (dp, 1 - mp)
        )

    def direct(k):
        to = (dp + k) % 16
        return remote(total.at[to], out_ref.at[dp], send.at[k], recv.at[k], (to, mp))

    order = list(range(1, 16)) + [0]
    for k in order:
        cross(k).start()
    for k in order:
        s = (dp + k) % 16
        cross(k).wait_recv()
        summed = (slab_ref[s, :, cols(mp)].astype(F32) + got[s].astype(F32)).astype(BF)
        if k == 0:
            out_ref[s] = summed
        else:
            total[s] = summed
            direct(k).start()
    for k in range(16):
        cross(k).wait_send()
    for k in range(1, 16):
        direct(k).wait()


def combine(slab):
    shape = (16, SLAB, slab.shape[2] // 2)
    return pl.pallas_call(
        combine_kernel,
        out_shape=jax.ShapeDtypeStruct(shape, BF),
        in_specs=[VM],
        out_specs=VM,
        scratch_shapes=[pltpu.VMEM(shape, BF), pltpu.VMEM(shape, BF)]
        + [pltpu.SemaphoreType.DMA((16,))] * 4,
        compiler_params=params(4),
    )(slab)


def swap_kernel(back_ref, layer_ref, gate_ref, back_out, layer_out, gate_out, own, send, recv):
    dp, mp = lax.axis_index("dp"), lax.axis_index("mp")
    half = back_ref.shape[1]
    rows = layer_out.shape[0]
    greet([(dp, 1 - mp)])
    mine = pl.ds(pl.multiple_of(mp * half, half), half)

    def part(m):
        return layer_ref.at[pl.ds(pl.multiple_of(m * rows, rows), rows), :]

    copies = [
        remote(gate_ref, gate_out, send.at[0], recv.at[0], (dp, 1 - mp)),
        remote(back_ref, back_out.at[:, mine], send.at[1], recv.at[1], (dp, 1 - mp)),
        remote(part(1 - mp), layer_out.at[:, mine], send.at[2], recv.at[2], (dp, 1 - mp)),
        pltpu.make_async_copy(back_ref, back_out.at[:, mine], own.at[0]),
        pltpu.make_async_copy(part(mp), layer_out.at[:, mine], own.at[1]),
    ]
    for c in copies:
        c.start()
    for c in copies:
        c.wait()


def swap(back, layer, gate):
    length, half = back.shape
    return pl.pallas_call(
        swap_kernel,
        out_shape=(
            jax.ShapeDtypeStruct((length, 2 * half), BF),
            jax.ShapeDtypeStruct((length // 2, 2 * half), BF),
            jax.ShapeDtypeStruct(gate.shape, F32),
        ),
        in_specs=[VM] * 3,
        out_specs=[VM] * 3,
        scratch_shapes=[
            pltpu.SemaphoreType.DMA((2,)),
            pltpu.SemaphoreType.DMA((3,)),
            pltpu.SemaphoreType.DMA((3,)),
        ],
        compiler_params=params(5),
    )(back, layer, gate)


def reduce_kernel(gw_ref, ga_ref, few_ref, sum_ref, ga_out, few_out, sib_got, x_got, up_got, down_got, acc, ga_got, sib_send, sib_recv, x_send, x_recv, z_send, z_recv, ga_send, ga_recv, few_got, few_part, few_mate, few_total, f1_send, f1_recv, f2_send, f2_recv, y_send, y_recv):
    dp, mp, z, x, core = place()
    sib = dp + 1 - 2 * core
    across = dp + 2 - 4 * x
    greet([((dp + k) % 16, mp) for k in range(1, 16)] + [(dp, 1 - mp)])

    def scatter(k):
        to = (dp + k) % 16
        return remote(few_ref.at[to], few_got.at[k], f1_send.at[k], f1_recv.at[k], (to, mp))

    def collect(k):
        to = (dp + k) % 16
        return remote(few_total, few_out.at[dp], f2_send.at[k], f2_recv.at[k], (to, mp))

    mate = remote(few_part, few_mate, y_send, y_recv, (dp, 1 - mp))

    def rows(b):
        return pl.ds(pl.multiple_of(b * 48, 48), 48)

    def to_sib(xx, zz):
        b = zz * 4 + xx * 2 + 1 - core
        j = xx * 4 + zz
        return remote(
            gw_ref.at[:, rows(b), :], sib_got.at[j], sib_send.at[j], sib_recv.at[j], (sib, mp)
        )

    def to_across(zz):
        return remote(acc.at[0, zz], x_got.at[zz], x_send.at[zz], x_recv.at[zz], (across, mp))

    def to_up(zz):
        return remote(acc.at[1, zz], up_got.at[zz], z_send.at[0, zz], z_recv.at[0, zz], (dp + 4, mp))

    def to_down(zz):
        return remote(
            acc.at[1, zz], down_got.at[zz], z_send.at[1, zz], z_recv.at[1, zz], (dp - 4, mp)
        )

    half = ga_out.shape[0]
    pair = remote(
        ga_ref.at[pl.ds(pl.multiple_of((1 - mp) * half, half), half), :],
        ga_got,
        ga_send,
        ga_recv,
        (dp, 1 - mp),
    )
    order = (0, 3, 1, 2)
    for zz in order:
        to_sib(1 - x, zz).start()
    for zz in order:
        to_sib(x, zz).start()
    pair.start()
    for k in range(1, 16):
        scatter(k).start()

    def own(b):
        return gw_ref[:, rows(b), :].astype(F32)

    for zz in order:
        to_sib(1 - x, zz).wait_recv()
        b = zz * 4 + (1 - x) * 2 + core
        acc[0, zz] = (own(b) + sib_got[(1 - x) * 4 + zz].astype(F32)).astype(BF)
        to_across(zz).start()
    total = few_ref[dp]
    for k in range(1, 16):
        scatter(k).wait_recv()
        total = total + few_got[k]
    few_part[...] = total
    mate.start()
    for zz in order:
        to_sib(x, zz).wait_recv()
    for zz in order:
        to_across(zz).wait_recv()
        b = zz * 4 + x * 2 + core
        part = own(b) + sib_got[x * 4 + zz].astype(F32) + x_got[zz].astype(F32)
        acc[1, zz] = part.astype(BF)

        @pl.when(jnp.logical_and(zz > z, z > 0))
        def _():
            to_up(zz).wait_recv()
            acc[1, zz] = (acc[1, zz].astype(F32) + up_got[zz].astype(F32)).astype(BF)

        @pl.when(jnp.logical_and(zz < z, z < 3))
        def _():
            to_down(zz).wait_recv()
            acc[1, zz] = (acc[1, zz].astype(F32) + down_got[zz].astype(F32)).astype(BF)

        @pl.when(zz > z)
        def _():
            to_up(zz).start()

        @pl.when(zz < z)
        def _():
            to_down(zz).start()

        @pl.when(zz == z)
        def _():
            sum_ref[...] = part

    mate.wait()
    few_total[...] = few_part[...] + few_mate[...]
    few_out[dp] = few_total[...]
    for k in range(1, 16):
        collect(k).start()

    @pl.when(z > 0)
    def _():
        to_up(z).wait_recv()
        sum_ref[...] += up_got[z].astype(F32)

    @pl.when(z < 3)
    def _():
        to_down(z).wait_recv()
        sum_ref[...] += down_got[z].astype(F32)

    pair.wait()
    ga_out[...] = (
        ga_ref[pl.ds(pl.multiple_of(mp * half, half), half), :].astype(F32)
        + ga_got[...].astype(F32)
    )
    for zz in range(4):
        to_sib(0, zz).wait_send()
        to_sib(1, zz).wait_send()
        to_across(zz).wait_send()

        @pl.when(zz > z)
        def _():
            to_up(zz).wait_send()

        @pl.when(zz < z)
        def _():
            to_down(zz).wait_send()
    for k in range(1, 16):
        scatter(k).wait_send()
        collect(k).wait()


def reduce_weights(gw, ga, arrays):
    kinds, _, width = gw.shape
    block = (kinds, 48, width)
    half = (ga.shape[0] // 2, ga.shape[1])
    flat = jnp.concatenate([a.reshape(-1) for a in arrays])
    rows = -(-flat.size // (16 * 8 * 128)) * 8
    few = jnp.pad(flat, (0, 16 * rows * 128 - flat.size)).reshape(16, rows, 128)
    dma = pltpu.SemaphoreType.DMA
    sums, ga_sum, out = pl.pallas_call(
        reduce_kernel,
        out_shape=(
            jax.ShapeDtypeStruct(block, F32),
            jax.ShapeDtypeStruct(half, F32),
            jax.ShapeDtypeStruct(few.shape, F32),
        ),
        in_specs=[VM] * 3,
        out_specs=[VM] * 3,
        scratch_shapes=[
            pltpu.VMEM((8,) + block, BF),
            pltpu.VMEM((4,) + block, BF),
            pltpu.VMEM((4,) + block, BF),
            pltpu.VMEM((4,) + block, BF),
            pltpu.VMEM((2, 4) + block, BF),
            pltpu.VMEM(half, BF),
            dma((8,)),
            dma((8,)),
            dma((4,)),
            dma((4,)),
            dma((2, 4)),
            dma((2, 4)),
            dma,
            dma,
            pltpu.VMEM(few.shape, F32),
            pltpu.VMEM((rows, 128), F32),
            pltpu.VMEM((rows, 128), F32),
            pltpu.VMEM((rows, 128), F32),
            dma((16,)),
            dma((16,)),
            dma((16,)),
            dma((16,)),
            dma,
            dma,
        ],
        compiler_params=params(6),
    )(gw, ga, few)
    out = out.reshape(-1)
    ends, at = [], 0
    for a in arrays:
        ends.append(out[at : at + a.size].reshape(a.shape))
        at += a.size
    return sums, ga_sum, ends


def local_pairs(
    tokens,
    w_query,
    w_key,
    w_value,
    w_output,
    bias_table,
    gain_attn,
    gain_moe,
    router,
    w_in,
    w_out,
    routes,
    slots,
    buckets,
    cotangent,
):
    length, width = tokens.shape
    half_rows, half = length // 2, width // 2
    mp_rank = lax.axis_index("mp")
    experts = router.shape[1]
    capacity = (5 * length + 4 * experts - 1) // (4 * experts)
    head_width = w_query.shape[1]
    heads = head_width // HEAD_DIM

    def own_rows(array):
        return lax.dynamic_slice_in_dim(array, mp_rank * half_rows, half_rows, 0)

    def own_cols(array):
        return lax.dynamic_slice_in_dim(array, mp_rank * half, half, 1)

    weights = gather_weights(jnp.stack([w_query, w_key, w_value, w_output.T]))
    bucket_hot = (
        buckets[:, None] == jnp.arange(bias_table.shape[0], dtype=jnp.int32)[None, :]
    ).astype(F32)
    bucket_hot = jnp.pad(bucket_hot, ((0, 1), (0, 0)))
    table_heads = lax.dynamic_slice_in_dim(bias_table, mp_rank * heads, heads, 1)
    table_heads = jnp.pad(table_heads, ((0, 0), (0, 8 - heads)))
    offsets = jnp.einsum("ob,bh->ho", bucket_hot, table_heads, precision=lax.Precision.HIGHEST)
    partial, normed_attn, qkv, context, chances = pl.pallas_call(
        lambda *refs: forward_kernel(heads, *refs),
        out_shape=(
            jax.ShapeDtypeStruct((length, width), BF),
            jax.ShapeDtypeStruct((length, width), BF),
            jax.ShapeDtypeStruct((3, length, head_width), BF),
            jax.ShapeDtypeStruct((length, head_width), BF),
            jax.ShapeDtypeStruct((heads, length, length), F32),
        ),
        in_specs=[VM] * 4,
        out_specs=[VM] * 5,
        compiler_params=params(),
    )(tokens, gain_attn[None, :], weights, offsets)
    inputs = tokens.astype(F32)
    residual = inputs + pair_sum(partial)
    moe_float, inverse_moe = normalize(residual, gain_moe)
    normed_moe = moe_float.astype(BF)
    logits = jnp.dot(normed_moe, router, preferred_element_type=F32)
    chance_all = jax.nn.softmax(logits, axis=-1)
    route_hot = (routes[:, None] == jnp.arange(experts, dtype=jnp.int32)[None, :]).astype(F32)
    gates = jnp.sum(chance_all * route_hot, axis=1)
    gradient = cotangent.astype(F32)
    grad_rows = (gates[:, None] * gradient).astype(BF)
    spots = jnp.arange(experts * SLAB, dtype=jnp.int32)[:, None]
    target = (routes * SLAB + slots)[None, :]
    hot_in = (spots == target).astype(BF)
    hot_grad = (spots == target + capacity).astype(BF)
    slab = jnp.dot(
        jnp.concatenate([hot_in, hot_grad], axis=1),
        jnp.concatenate([own_cols(normed_moe), own_cols(grad_rows)], axis=0),
        preferred_element_type=F32,
    ).astype(BF)
    arrived = dispatch(slab.reshape(experts, SLAB, half))
    back_slab, grad_w_in, grad_w_out = expert_layer(arrived, w_in, w_out, capacity)
    returned = combine(back_slab).reshape(experts * SLAB, half)
    expert_rows = dot(hot_in, returned, (0, 0))
    back_half = dot(hot_grad, returned, (0, 0)).astype(BF)
    layer_half = (own_cols(residual) + gates[:, None] * expert_rows).astype(BF)
    gate_half = jnp.sum(own_cols(gradient) * expert_rows, axis=1)
    grad_slots, layer_out, gate_other = swap(
        back_half, layer_half, jnp.broadcast_to(gate_half[None, :], (8, length))
    )
    grad_gates = gate_half + gate_other[0]
    grad_logits = (grad_gates[:, None] * gates[:, None] * (route_hot - chance_all)).astype(BF)
    grad_normed = grad_slots.astype(F32) + jnp.einsum(
        "se,de->sd", grad_logits, router, preferred_element_type=F32
    )
    grad_residual = gradient + norm_backward(residual, inverse_moe, gain_moe, grad_normed)
    grad_gain_moe = jnp.sum(own_rows(grad_normed) * own_rows(residual * inverse_moe), axis=0)
    grad_router = jnp.einsum(
        "sd,se->de", own_rows(normed_moe), own_rows(grad_logits), preferred_element_type=F32
    )
    grad_weights, grad_attn, grad_offsets = pl.pallas_call(
        lambda *refs: backward_kernel(heads, *refs),
        out_shape=(
            jax.ShapeDtypeStruct(weights.shape, BF),
            jax.ShapeDtypeStruct((length, width), BF),
            jax.ShapeDtypeStruct((8, 2 * length), F32),
        ),
        in_specs=[VM] * 6,
        out_specs=[VM] * 3,
        scratch_shapes=[
            pltpu.VMEM((length, head_width), BF),
            pltpu.VMEM((3, length, head_width), BF),
        ],
        compiler_params=params(),
    )(grad_residual.astype(BF), normed_attn, weights, qkv, context, chances)
    inverse_attn = lax.rsqrt(jnp.mean(inputs * inputs, axis=-1, keepdims=True) + EPS)
    grad_gain_attn = jnp.sum(grad_attn.astype(F32) * inputs * inverse_attn, axis=0)
    table_part = jnp.einsum(
        "ob,ho->bh", bucket_hot, grad_offsets, precision=lax.Precision.HIGHEST
    )[:, :heads]
    table_full = lax.dynamic_update_slice_in_dim(
        jnp.zeros(bias_table.shape, F32), table_part, mp_rank * heads, 1
    )
    sums, own_grad_attn, (grad_table, gain_attn_total, gain_moe_total, router_total) = (
        reduce_weights(
            grad_weights, grad_attn, [table_full, grad_gain_attn, grad_gain_moe, grad_router]
        )
    )
    input_grad = own_rows(grad_residual) + norm_backward(
        own_rows(inputs), own_rows(inverse_attn), gain_attn, own_grad_attn
    )
    return (
        layer_out,
        input_grad,
        sums[0],
        sums[1],
        sums[2],
        sums[3].T,
        grad_table,
        gain_attn_total,
        gain_moe_total,
        router_total,
        grad_w_in,
        grad_w_out,
    )


def solution(mesh):
    in_specs = (
        P("dp", None),
        P("dp", "mp"),
        P("dp", "mp"),
        P("dp", "mp"),
        P("mp", "dp"),
        P(),
        P(),
        P(),
        P(),
        P("dp", None, "mp"),
        P("dp", "mp", None),
        P("dp"),
        P("dp"),
        P(),
        P("dp", None),
    )
    out_specs = (
        P(("dp", "mp"), None),
        P(("dp", "mp"), None),
        P("dp", "mp"),
        P("dp", "mp"),
        P("dp", "mp"),
        P("mp", "dp"),
        P(),
        P(),
        P(),
        P(),
        P("dp", None, "mp"),
        P("dp", "mp", None),
    )
    small = mesh.shape["mp"] == 2 and mesh.shape["dp"] == 16
    return jax.shard_map(local_pairs if small else local, mesh=mesh, in_specs=in_specs, out_specs=out_specs, check_vma=False)
```

```python
import jax
import jax.numpy as jnp
from jax import lax
from jax.experimental import pallas as pl
from jax.experimental.pallas import tpu as pltpu
from jax.sharding import PartitionSpec as P

HEAD_DIM = 64


EPS = 1e-06
query_rows = 512


def in_blocks(array, dim, count):
    lengths = array.shape
    tiles = array.reshape(*lengths[:dim], count, lengths[dim] // count, *lengths[dim + 1 :])
    return jnp.moveaxis(tiles, dim, 0)


def sum_at_owner(array, axis, dim):
    count = lax.axis_size(axis)
    tiles = lax.all_to_all(in_blocks(array, dim, count), axis, 0, 0, tiled=True)
    return jnp.sum(tiles.astype(jnp.float32), axis=0)


def in_one_piece(arrays, axis, dim, along):
    ends, at = ([], 0)
    for a in arrays[:-1]:
        at += a.shape[along]
        ends.append(at)
    both = jnp.concatenate(arrays, axis=along)
    return tuple(jnp.split(sum_at_owner(both, axis, dim), ends, axis=along))


def normalize(inputs, gains):
    inverse = lax.rsqrt(jnp.mean(inputs * inputs, axis=-1, keepdims=True) + EPS)
    return (inputs * inverse * gains, inverse)


def norm_backward(inputs, inverse, gains, gradient):
    unit_rows = inputs * inverse
    scaled = gradient * gains
    return inverse * (scaled - unit_rows * jnp.mean(unit_rows * scaled, axis=-1, keepdims=True))


def offset_band(offset_bias, row_count, key_count):
    head_count = offset_bias.shape[0]
    window = offset_bias
    window = jnp.concatenate([window, jnp.zeros((head_count, 1), window.dtype)], axis=1)
    turned = jnp.concatenate([window[:, row_count - 1 :], window[:, : row_count - 1]], axis=1)
    span = row_count + key_count - 1
    repeated = jnp.tile(turned, (1, row_count))[:, : row_count * span]
    return repeated.reshape(head_count, row_count, span)[:, :, :key_count]


def band_sums(gradient, row_count, key_count):
    head_count = gradient.shape[0]
    padded = jnp.concatenate(
        [jnp.zeros((head_count, row_count, row_count), gradient.dtype), gradient], axis=2
    )
    flattened = jnp.concatenate(
        [padded.reshape(head_count, -1), jnp.zeros((head_count, row_count), gradient.dtype)], axis=1
    )
    skewed = flattened.reshape(head_count, row_count, row_count + key_count + 1)
    return jnp.sum(skewed, axis=1)[:, 1 : row_count + key_count]


def local(
    tokens,
    w_query,
    w_key,
    w_value,
    w_output,
    bias_table,
    gain_attn,
    gain_moe,
    router,
    w_in,
    w_out,
    routes,
    slots,
    buckets,
    cotangent,
):
    length, model_width = tokens.shape
    mp_count = lax.axis_size("mp")
    mp_rank = lax.axis_index("mp")
    own_rows = length // mp_count
    own_first = mp_rank * own_rows
    experts = router.shape[1]
    capacity = (5 * length + 4 * experts - 1) // (4 * experts)
    head_width = w_query.shape[1]
    head_count = head_width // HEAD_DIM
    row_block = min(query_rows, length)
    block_count = length // row_block
    block_starts = jnp.arange(block_count, dtype=jnp.int32) * row_block

    def own_slice(array):
        return lax.dynamic_slice_in_dim(array, own_first, own_rows, 0)

    inputs = tokens.astype(jnp.float32)
    normed_float, inverse_attn = normalize(inputs, gain_attn)
    normed_attn = normed_float.astype(jnp.bfloat16)
    full_query, full_key, full_value, full_output = (
        lax.all_gather(w_query, "dp", axis=0, tiled=True),
        lax.all_gather(w_key, "dp", axis=0, tiled=True),
        lax.all_gather(w_value, "dp", axis=0, tiled=True),
        lax.all_gather(w_output, "dp", axis=1, tiled=True),
    )
    w_joint = jnp.concatenate([full_query, full_key, full_value], axis=1)
    projected = jnp.dot(normed_attn, w_joint, preferred_element_type=jnp.float32).astype(
        jnp.bfloat16
    )
    queries = projected[:, :head_width].reshape(length, head_count, HEAD_DIM)
    keys_all = projected[:, head_width : 2 * head_width].reshape(length, head_count, HEAD_DIM)
    values = projected[:, 2 * head_width :].reshape(length, head_count, HEAD_DIM)
    bucket_hot = (
        buckets[:, None] == jnp.arange(bias_table.shape[0], dtype=jnp.int32)[None, :]
    ).astype(jnp.float32)
    table_heads = lax.dynamic_slice_in_dim(bias_table, mp_rank * head_count, head_count, 1)
    offset_bias = jnp.einsum("ob,bh->ho", bucket_hot, table_heads, precision=lax.Precision.HIGHEST)

    def attend_block(first_row):
        scores = jnp.einsum(
            "qhd,khd->hqk", queries, keys_all, preferred_element_type=jnp.float32
        ) + offset_band(offset_bias, row_block, length)
        peak_score = jnp.max(scores, axis=-1, keepdims=True)
        weights = jnp.exp(scores - peak_score)
        summed = jnp.sum(weights, axis=-1, keepdims=True)
        chances = (weights / summed).astype(jnp.bfloat16)
        context_rows = jnp.einsum(
            "hqk,khd->qhd", chances, values, preferred_element_type=jnp.float32
        )
        return (context_rows.astype(jnp.bfloat16), (peak_score + jnp.log(summed))[:, :, 0])

    context_blocks, log_totals = lax.map(attend_block, block_starts)
    context = context_blocks.reshape(length, head_width)
    partial_attn = jnp.dot(context, full_output, preferred_element_type=jnp.float32)
    attended = lax.psum(partial_attn.astype(jnp.bfloat16), "mp").astype(jnp.float32)
    residual = inputs + attended
    moe_float, inverse_moe = normalize(residual, gain_moe)
    normed_moe = moe_float.astype(jnp.bfloat16)
    logits = jnp.dot(normed_moe, router, preferred_element_type=jnp.float32)
    chance_all = jax.nn.softmax(logits, axis=-1)
    route_hot = (routes[:, None] == jnp.arange(experts, dtype=jnp.int32)[None, :]).astype(
        jnp.float32
    )
    gates = jnp.sum(chance_all * route_hot, axis=1)
    target = routes * capacity + slots
    slotted = (
        jnp.zeros((experts * capacity, model_width), jnp.bfloat16)
        .at[target]
        .set(normed_moe)
        .reshape(experts, capacity, model_width)
    )
    arrived = lax.all_to_all(slotted, "dp", split_axis=0, concat_axis=0, tiled=True)
    expert_input = arrived.reshape(-1, model_width)
    hidden_pre = jnp.dot(expert_input, w_in[0], preferred_element_type=jnp.float32)
    gelu_value, gelu_back = jax.vjp(lambda inner: jax.nn.gelu(inner, approximate=False), hidden_pre)
    hidden = gelu_value.astype(jnp.bfloat16)
    partial_out = jnp.dot(hidden, w_out[0], preferred_element_type=jnp.float32).reshape(
        arrived.shape
    )
    summed_out = lax.psum(partial_out.astype(jnp.bfloat16), "mp")
    returned = lax.all_to_all(summed_out, "dp", split_axis=0, concat_axis=0, tiled=True)
    expert_rows = returned.reshape(experts * capacity, model_width)[target].astype(jnp.float32)
    layer_full = residual + gates[:, None] * expert_rows
    layer_out = own_slice(layer_full).astype(jnp.bfloat16)
    gradient = cotangent.astype(jnp.float32)
    grad_gates = jnp.sum(gradient * expert_rows, axis=1)
    grad_rows = (gates[:, None] * gradient).astype(jnp.bfloat16)
    grad_slotted = (
        jnp.zeros((experts * capacity, model_width), jnp.bfloat16)
        .at[target]
        .set(grad_rows)
        .reshape(experts, capacity, model_width)
    )
    grad_arrived = lax.all_to_all(grad_slotted, "dp", split_axis=0, concat_axis=0, tiled=True)
    grad_expert = grad_arrived.reshape(-1, model_width)
    grad_hidden = jnp.einsum("rd,fd->rf", grad_expert, w_out[0], preferred_element_type=jnp.float32)
    grad_pre = gelu_back(grad_hidden)[0].astype(jnp.bfloat16)
    grad_w_out = jnp.einsum("rf,rd->fd", hidden, grad_expert, preferred_element_type=jnp.float32)[
        None
    ]
    grad_w_in = jnp.einsum("rd,rf->df", expert_input, grad_pre, preferred_element_type=jnp.float32)[
        None
    ]
    partial_back = jnp.einsum(
        "rf,df->rd", grad_pre, w_in[0], preferred_element_type=jnp.float32
    ).reshape(arrived.shape)
    grad_input_slots = lax.psum(partial_back.astype(jnp.bfloat16), "mp")
    grad_sent = lax.all_to_all(grad_input_slots, "dp", split_axis=0, concat_axis=0, tiled=True)
    grad_normed = grad_sent.reshape(experts * capacity, model_width)[target].astype(jnp.float32)
    grad_logits = (grad_gates[:, None] * gates[:, None] * (route_hot - chance_all)).astype(
        jnp.bfloat16
    )
    grad_normed = grad_normed + jnp.einsum(
        "se,de->sd", grad_logits, router, preferred_element_type=jnp.float32
    )
    grad_residual = gradient + norm_backward(residual, inverse_moe, gain_moe, grad_normed)
    grad_gain_moe = jnp.sum(own_slice(grad_normed) * own_slice(residual * inverse_moe), axis=0)
    grad_router = jnp.einsum(
        "sd,se->de",
        own_slice(normed_moe),
        own_slice(grad_logits),
        preferred_element_type=jnp.float32,
    )
    grad_attended = grad_residual.astype(jnp.bfloat16)
    grad_output = jnp.einsum(
        "sk,sd->kd", context, grad_attended, preferred_element_type=jnp.float32
    )
    grad_context = (
        jnp.einsum("sd,kd->sk", grad_attended, full_output, preferred_element_type=jnp.float32)
        .astype(jnp.bfloat16)
        .reshape(length, head_count, HEAD_DIM)
    )

    def back_block(running, items):
        first_row, log_total = items
        grad_keys, grad_values, grad_offsets = running
        scores = jnp.einsum(
            "qhd,khd->hqk", queries, keys_all, preferred_element_type=jnp.float32
        ) + offset_band(offset_bias, row_block, length)
        chances = jnp.exp(scores - log_total[:, :, None])
        grad_chances = jnp.einsum(
            "qhd,khd->hqk", grad_context, values, preferred_element_type=jnp.float32
        )
        grad_scores = chances * (
            grad_chances - jnp.sum(grad_chances * chances, axis=-1, keepdims=True)
        )
        grad_offsets = grad_offsets + band_sums(grad_scores, row_block, length)
        grad_low = grad_scores.astype(jnp.bfloat16)
        grad_queries = jnp.einsum(
            "hqk,khd->qhd", grad_low, keys_all, preferred_element_type=jnp.float32
        )
        grad_keys = grad_keys + jnp.einsum(
            "hqk,qhd->khd", grad_low, queries, preferred_element_type=jnp.float32
        )
        grad_values = grad_values + jnp.einsum(
            "hqk,qhd->khd",
            chances.astype(jnp.bfloat16),
            grad_context,
            preferred_element_type=jnp.float32,
        )
        return ((grad_keys, grad_values, grad_offsets), grad_queries.astype(jnp.bfloat16))

    zero_heads = jnp.zeros((length, head_count, HEAD_DIM), jnp.float32)
    zero_offsets = jnp.zeros((head_count, 2 * length - 1), jnp.float32)
    (grad_keys, grad_values, grad_offsets), grad_queries = lax.scan(
        back_block, (zero_heads, zero_heads, zero_offsets), (block_starts, log_totals)
    )
    grad_joint = jnp.concatenate(
        [
            grad_queries.reshape(length, head_width),
            grad_keys.astype(jnp.bfloat16).reshape(length, head_width),
            grad_values.astype(jnp.bfloat16).reshape(length, head_width),
        ],
        axis=1,
    )
    grad_weights = jnp.einsum(
        "sd,sk->dk", normed_attn, grad_joint, preferred_element_type=jnp.float32
    )
    grad_query, grad_key, grad_value, grad_out_proj = (
        *in_one_piece(
            (
                grad_weights[:, :head_width].astype(jnp.bfloat16),
                grad_weights[:, head_width : 2 * head_width].astype(jnp.bfloat16),
                grad_weights[:, 2 * head_width :].astype(jnp.bfloat16),
            ),
            "dp",
            0,
            1,
        ),
        sum_at_owner(grad_output.astype(jnp.bfloat16), "dp", 1),
    )
    own_grad_attn = lax.psum_scatter(
        jnp.einsum("sk,dk->sd", grad_joint, w_joint, preferred_element_type=jnp.float32).astype(
            jnp.bfloat16
        ),
        "mp",
        scatter_dimension=0,
        tiled=True,
    ).astype(jnp.float32)
    own_inputs = own_slice(inputs)
    own_inverse = own_slice(inverse_attn)
    input_grad = own_slice(grad_residual) + norm_backward(
        own_inputs, own_inverse, gain_attn, own_grad_attn
    )
    grad_gain_attn = jnp.sum(own_grad_attn * own_inputs * own_inverse, axis=0)
    table_part = jnp.einsum("ob,ho->bh", bucket_hot, grad_offsets, precision=lax.Precision.HIGHEST)
    table_full = lax.dynamic_update_slice_in_dim(
        jnp.zeros(bias_table.shape, jnp.float32), table_part, mp_rank * head_count, 1
    )
    grad_table, gain_attn_total, gain_moe_total, router_total = lax.psum(
        (table_full, grad_gain_attn, grad_gain_moe, grad_router), ("dp", "mp")
    )
    return (
        layer_out,
        input_grad,
        grad_query,
        grad_key,
        grad_value,
        grad_out_proj,
        grad_table,
        gain_attn_total,
        gain_moe_total,
        router_total,
        grad_w_in,
        grad_w_out,
    )


BF = jnp.bfloat16
F32 = jnp.float32
MESH = pl.DeviceIdType.MESH
VM = pl.BlockSpec(memory_space=pltpu.VMEM)
SLAB = 48


def params(collective_id=None):
    if collective_id is None:
        return pltpu.CompilerParams(vmem_limit_bytes=48 * 2**20)
    return pltpu.CompilerParams(
        vmem_limit_bytes=48 * 2**20, collective_id=collective_id, has_side_effects=True
    )


def dot(a, b, dims):
    return lax.dot_general(a, b, ((dims[:1], dims[1:]), ((), ())), preferred_element_type=F32)


def greet(devices):
    barrier = pltpu.get_barrier_semaphore()
    for device in devices:
        pl.semaphore_signal(barrier, inc=1, device_id=device, device_id_type=MESH)
    pl.semaphore_wait(barrier, len(devices))


def remote(src, dst, send, recv, device):
    return pltpu.make_async_remote_copy(
        src_ref=src, dst_ref=dst, send_sem=send, recv_sem=recv, device_id=device, device_id_type=MESH
    )


def place():
    dp = lax.axis_index("dp")
    return dp, lax.axis_index("mp"), dp // 4, (dp // 2) % 2, dp % 2


def gather_kernel(own_ref, out_ref, own_sem, send, recv):
    dp, mp, z, x, core = place()
    sib = dp + 1 - 2 * core
    across = dp + 2 - 4 * x
    barrier = pltpu.get_barrier_semaphore()
    for other in (sib, across):
        pl.semaphore_signal(barrier, inc=1, device_id=(other, mp), device_id_type=MESH)

    @pl.when(z > 0)
    def _():
        pl.semaphore_signal(barrier, inc=1, device_id=(dp - 4, mp), device_id_type=MESH)

    @pl.when(z < 3)
    def _():
        pl.semaphore_signal(barrier, inc=1, device_id=(dp + 4, mp), device_id_type=MESH)

    pl.semaphore_wait(barrier, 2 + jnp.minimum(z, 1) + jnp.minimum(3 - z, 1))

    def block(b):
        return out_ref.at[:, pl.ds(pl.multiple_of(b * 48, 48), 48), :]

    def copy(b, way, device, src=None):
        return remote(
            block(b) if src is None else src, block(b), send.at[way, b], recv.at[b], (device, mp)
        )

    own = pltpu.make_async_copy(own_ref, block(dp), own_sem)
    own.start()

    def spread(b, src, up, down):
        @pl.when(jnp.logical_and(up, z < 3))
        def _():
            copy(b, 0, dp + 4, src).start()

        @pl.when(jnp.logical_and(down, z > 0))
        def _():
            copy(b, 1, dp - 4, src).start()

        copy(b, 2, across, src).start()
        copy(b, 3, sib, src).start()

    spread(dp, own_ref, True, True)
    for s in (1, 2, 3):

        @pl.when(z - s >= 0)
        def _():
            b = dp - 4 * s
            copy(b, 0, sib).wait_recv()
            spread(b, None, True, False)

        @pl.when(z + s <= 3)
        def _():
            b = dp + 4 * s
            copy(b, 0, sib).wait_recv()
            spread(b, None, False, True)

    for s in range(4):
        for sign in (1, -1) if s else (1,):

            @pl.when(jnp.logical_and(z + sign * s >= 0, z + sign * s <= 3))
            def _():
                b = across + 4 * s * sign
                copy(b, 0, sib).wait_recv()
                copy(b, 3, sib).start()

    for zz in range(4):
        for xx in range(2):
            copy(zz * 4 + xx * 2 + 1 - core, 3, sib).wait_recv()
    own.wait()
    for zz in range(4):
        b = zz * 4 + x * 2 + core

        @pl.when(jnp.logical_and(zz <= z, z < 3))
        def _():
            copy(b, 0, sib).wait_send()

        @pl.when(jnp.logical_and(zz >= z, z > 0))
        def _():
            copy(b, 1, sib).wait_send()

        copy(b, 2, sib).wait_send()
        copy(b, 3, sib).wait_send()
        copy(zz * 4 + (1 - x) * 2 + core, 3, sib).wait_send()


def gather_weights(own):
    return pl.pallas_call(
        gather_kernel,
        out_shape=jax.ShapeDtypeStruct((own.shape[0], 768, own.shape[2]), BF),
        in_specs=[VM],
        out_specs=VM,
        scratch_shapes=[
            pltpu.SemaphoreType.DMA,
            pltpu.SemaphoreType.DMA((4, 16)),
            pltpu.SemaphoreType.DMA((16,)),
        ],
        compiler_params=params(1),
    )(own)


def forward_kernel(heads, tokens_ref, gain_ref, w_ref, off_ref, part_ref, normed_ref, qkv_ref, ctx_ref, p_ref):
    x = tokens_ref[...].astype(F32)
    normed = normalize(x, gain_ref[...])[0].astype(BF)
    normed_ref[...] = normed
    for j in range(3):
        qkv_ref[j] = dot(normed, w_ref[j], (1, 0)).astype(BF)
    length = x.shape[0]
    for h in range(heads):
        cols = slice(h * HEAD_DIM, (h + 1) * HEAD_DIM)
        row = jnp.broadcast_to(off_ref[h : h + 1, :], (length, 2 * length))
        bias = pltpu.roll(row, length + 1, 1, stride=1, stride_axis=0)[:, :length]
        scores = dot(qkv_ref[0, :, cols], qkv_ref[1, :, cols], (1, 1)) + bias
        weights = jnp.exp(scores - jnp.max(scores, axis=-1, keepdims=True))
        chances = weights / jnp.sum(weights, axis=-1, keepdims=True)
        p_ref[h] = chances
        ctx_ref[:, cols] = dot(chances.astype(BF), qkv_ref[2, :, cols], (1, 0)).astype(BF)
    part_ref[...] = dot(ctx_ref[...], w_ref[3], (1, 1)).astype(BF)


def backward_kernel(heads, g_ref, normed_ref, w_ref, qkv_ref, ctx_ref, p_ref, gw_ref, ga_ref, goff_ref, gc_ref, gj_ref):
    length = g_ref.shape[0]
    grad = g_ref[...]
    gw_ref[3] = dot(grad, ctx_ref[...], (0, 0)).astype(BF)
    gc_ref[...] = dot(grad, w_ref[3], (1, 0)).astype(BF)
    flip = (
        lax.broadcasted_iota(jnp.int32, (length, length), 0)
        + lax.broadcasted_iota(jnp.int32, (length, length), 1)
        == length - 1
    ).astype(F32).astype(BF)
    zeros = jnp.zeros((length, length), F32)
    goff_ref[...] = jnp.zeros_like(goff_ref)
    for h in range(heads):
        cols = slice(h * HEAD_DIM, (h + 1) * HEAD_DIM)
        chances = p_ref[h]
        gctx = gc_ref[:, cols]
        grad_chances = dot(gctx, qkv_ref[2, :, cols], (1, 1))
        grad_scores = chances * (
            grad_chances - jnp.sum(grad_chances * chances, axis=-1, keepdims=True)
        )
        high = grad_scores.astype(BF)
        rest = (grad_scores - high.astype(F32)).astype(BF)
        flipped = dot(flip, high, (1, 0)) + dot(flip, rest, (1, 0))
        skewed = pltpu.roll(
            jnp.concatenate([flipped, zeros], axis=1), 0, 1, stride=1, stride_axis=0
        )
        goff_ref[h : h + 1, :] = jnp.sum(skewed, axis=0, keepdims=True)
        gj_ref[0, :, cols] = dot(high, qkv_ref[1, :, cols], (1, 0)).astype(BF)
        gj_ref[1, :, cols] = dot(high, qkv_ref[0, :, cols], (0, 0)).astype(BF)
        gj_ref[2, :, cols] = dot(chances.astype(BF), gctx, (0, 0)).astype(BF)
    total = None
    for j in range(3):
        gw_ref[j] = dot(normed_ref[...], gj_ref[j], (0, 0)).astype(BF)
        term = dot(gj_ref[j], w_ref[j], (1, 1))
        total = term if total is None else total + term
    ga_ref[...] = total.astype(BF)


def pair_kernel(a_ref, o_ref, got, send, recv):
    dp, mp = lax.axis_index("dp"), lax.axis_index("mp")
    greet([(dp, 1 - mp)])
    c = remote(a_ref, got, send, recv, (dp, 1 - mp))
    c.start()
    c.wait()
    o_ref[...] = a_ref[...].astype(F32) + got[...].astype(F32)


def pair_sum(a):
    return pl.pallas_call(
        pair_kernel,
        out_shape=jax.ShapeDtypeStruct(a.shape, F32),
        in_specs=[VM],
        out_specs=VM,
        scratch_shapes=[pltpu.VMEM(a.shape, a.dtype), pltpu.SemaphoreType.DMA, pltpu.SemaphoreType.DMA],
        compiler_params=params(2),
    )(a)


def dispatch_kernel(slab_ref, out_ref, own_sem, send, recv, ysend, yrecv):
    dp, mp = lax.axis_index("dp"), lax.axis_index("mp")
    half = slab_ref.shape[2]
    greet([((dp + k) % 16, mp) for k in range(1, 16)] + [(dp, 1 - mp)])

    def peer(k):
        return dp + sum(bit * (1 - 2 * (dp // bit % 2)) for bit in (1, 2, 4, 8) if k & bit)

    def spot(s, m):
        return out_ref.at[s, :, pl.ds(pl.multiple_of(m * half, half), half)]

    own = pltpu.make_async_copy(slab_ref.at[dp], spot(dp, mp), own_sem)
    own.start()

    def cross(k):
        s = peer(k)
        src = slab_ref.at[dp] if k == 0 else spot(s, mp)
        return remote(src, spot(s, mp), ysend.at[k], yrecv.at[k], (dp, 1 - mp))

    def direct(k):
        to = peer(k)
        return remote(slab_ref.at[to], spot(dp, mp), send.at[k], recv.at[k], (to, mp))

    for k in (8, 1, 12, 2, 9, 3, 13, 4, 10, 5, 14, 6, 11, 7, 15):
        direct(k).start()
    cross(0).start()
    for k in range(1, 16):
        direct(k).wait_recv()
        cross(k).start()
    for k in range(16):
        cross(k).wait()
    for k in range(1, 16):
        direct(k).wait_send()
    own.wait()


def dispatch(slab):
    return pl.pallas_call(
        dispatch_kernel,
        out_shape=jax.ShapeDtypeStruct((16, SLAB, 2 * slab.shape[2]), BF),
        in_specs=[VM],
        out_specs=VM,
        scratch_shapes=[pltpu.SemaphoreType.DMA] + [pltpu.SemaphoreType.DMA((16,))] * 4,
        compiler_params=params(3),
    )(slab)


def expert_kernel(capacity, arrived_ref, w_in_ref, w_out_ref, slab_ref, gin_ref, gout_ref, x_ref, g_ref, out_ref, back_ref):
    step, last = pl.program_id(0), pl.num_programs(0) - 1
    packed = x_ref.shape[0]
    count = packed // capacity

    def chooser(first):
        row = lax.broadcasted_iota(jnp.int32, (packed, count * SLAB), 0)
        col = lax.broadcasted_iota(jnp.int32, (packed, count * SLAB), 1)
        return (col == row + row // capacity * (SLAB - capacity) + first).astype(F32).astype(BF)

    @pl.when(step == 0)
    def _():
        x_ref[...] = dot(chooser(0), arrived_ref[...], (1, 0)).astype(BF)
        g_ref[...] = dot(chooser(capacity), arrived_ref[...], (1, 0)).astype(BF)
        out_ref[...] = jnp.zeros_like(out_ref)
        back_ref[...] = jnp.zeros_like(back_ref)

    pre = dot(x_ref[...], w_in_ref[0], (1, 0))
    share = 0.5 * (1.0 + lax.erf(pre * (0.5**0.5)))
    hidden = (pre * share).astype(BF)
    slope = share + pre * jnp.exp(-0.5 * pre * pre) * ((0.5 / jnp.pi) ** 0.5)
    out_ref[...] += dot(hidden, w_out_ref[0], (1, 0))
    grad_pre = (slope * dot(g_ref[...], w_out_ref[0], (1, 1))).astype(BF)
    back_ref[...] += dot(grad_pre, w_in_ref[0], (1, 1))
    gout_ref[0] = dot(hidden, g_ref[...], (0, 0))
    gin_ref[0] = dot(x_ref[...], grad_pre, (0, 0))

    @pl.when(step == last)
    def _():
        slab_ref[...] = (
            dot(chooser(0), out_ref[...].astype(BF), (0, 0))
            + dot(chooser(capacity), back_ref[...].astype(BF), (0, 0))
        ).astype(BF)


def expert_layer(arrived, w_in, w_out, capacity):
    count, _, width = arrived.shape
    inner = w_in.shape[2]
    tile = 256
    packed = count * capacity
    whole = pl.BlockSpec((count * SLAB, width), lambda i: (0, 0))
    in_tile = pl.BlockSpec((1, width, tile), lambda i: (0, 0, i))
    out_tile = pl.BlockSpec((1, tile, width), lambda i: (0, i, 0))
    slab, gin, gout = pl.pallas_call(
        lambda *refs: expert_kernel(capacity, *refs),
        grid=(inner // tile,),
        out_shape=(
            jax.ShapeDtypeStruct((count * SLAB, width), BF),
            jax.ShapeDtypeStruct(w_in.shape, F32),
            jax.ShapeDtypeStruct(w_out.shape, F32),
        ),
        in_specs=[whole, in_tile, out_tile],
        out_specs=(whole, in_tile, out_tile),
        scratch_shapes=[
            pltpu.VMEM((packed, width), BF),
            pltpu.VMEM((packed, width), BF),
            pltpu.VMEM((packed, width), F32),
            pltpu.VMEM((packed, width), F32),
        ],
        compiler_params=params(),
    )(arrived.reshape(count * SLAB, width), w_in, w_out)
    return slab.reshape(arrived.shape), gin, gout


def combine_kernel(slab_ref, out_ref, got, total, send, recv, ysend, yrecv):
    dp, mp = lax.axis_index("dp"), lax.axis_index("mp")
    half = out_ref.shape[2]
    greet([((dp + k) % 16, mp) for k in range(1, 16)] + [(dp, 1 - mp)])

    def peer(k):
        return dp + sum(bit * (1 - 2 * (dp // bit % 2)) for bit in (1, 2, 4, 8) if k & bit)

    def cols(m):
        return pl.ds(pl.multiple_of(m * half, half), half)

    def cross(k):
        s = peer(k)
        return remote(
            slab_ref.at[s, :, cols(1 - mp)], got.at[s], ysend.at[k], yrecv.at[k], (dp, 1 - mp)
        )

    def direct(k):
        to = peer(k)
        return remote(total.at[to], out_ref.at[dp], send.at[k], recv.at[k], (to, mp))

    order = (12, 8, 13, 9, 14, 10, 15, 11, 4, 5, 6, 7, 2, 3, 1, 0)
    for k in order:
        cross(k).start()
    for k in order:
        s = peer(k)
        cross(k).wait_recv()
        summed = (slab_ref[s, :, cols(mp)].astype(F32) + got[s].astype(F32)).astype(BF)
        if k == 0:
            out_ref[s] = summed
        else:
            total[s] = summed
            direct(k).start()
    for k in range(16):
        cross(k).wait_send()
    for k in range(1, 16):
        direct(k).wait()


def combine(slab):
    shape = (16, SLAB, slab.shape[2] // 2)
    return pl.pallas_call(
        combine_kernel,
        out_shape=jax.ShapeDtypeStruct(shape, BF),
        in_specs=[VM],
        out_specs=VM,
        scratch_shapes=[pltpu.VMEM(shape, BF), pltpu.VMEM(shape, BF)]
        + [pltpu.SemaphoreType.DMA((16,))] * 4,
        compiler_params=params(4),
    )(slab)


def swap_kernel(back_ref, gate_ref, back_out, gate_out, own, send, recv):
    dp, mp = lax.axis_index("dp"), lax.axis_index("mp")
    half = back_ref.shape[1]
    greet([(dp, 1 - mp)])
    mine = back_out.at[:, pl.ds(pl.multiple_of(mp * half, half), half)]
    copies = [
        remote(gate_ref, gate_out, send.at[0], recv.at[0], (dp, 1 - mp)),
        remote(back_ref, mine, send.at[1], recv.at[1], (dp, 1 - mp)),
        pltpu.make_async_copy(back_ref, mine, own),
    ]
    for c in copies:
        c.start()
    for c in copies:
        c.wait()


def swap(back, gate):
    length, half = back.shape
    return pl.pallas_call(
        swap_kernel,
        out_shape=(
            jax.ShapeDtypeStruct((length, 2 * half), BF),
            jax.ShapeDtypeStruct(gate.shape, F32),
        ),
        in_specs=[VM] * 2,
        out_specs=[VM] * 2,
        scratch_shapes=[
            pltpu.SemaphoreType.DMA,
            pltpu.SemaphoreType.DMA((2,)),
            pltpu.SemaphoreType.DMA((2,)),
        ],
        compiler_params=params(5),
    )(back, gate)


def reduce_kernel(gw_ref, ga_ref, few_ref, layer_ref, sum_ref, ga_out, few_out, layer_out, sib_got, x_got, up_got, down_got, acc, ga_got, sib_send, sib_recv, x_send, x_recv, z_send, z_recv, ga_send, ga_recv, few_got, few_part, few_mate, few_total, f1_send, f1_recv, f2_send, f2_recv, y_send, y_recv, own_sem):
    dp, mp, z, x, core = place()
    sib = dp + 1 - 2 * core
    across = dp + 2 - 4 * x
    greet([((dp + k) % 16, mp) for k in range(1, 16)] + [(dp, 1 - mp)])

    def scatter(k):
        to = (dp + k) % 16
        return remote(few_ref.at[to], few_got.at[k], f1_send.at[k], f1_recv.at[k], (to, mp))

    def collect(k):
        to = (dp + k) % 16
        return remote(few_total, few_out.at[dp], f2_send.at[k], f2_recv.at[k], (to, mp))

    mate = remote(few_part, few_mate, y_send, y_recv, (dp, 1 - mp))

    def rows(b):
        return pl.ds(pl.multiple_of(b * 48, 48), 48)

    def to_sib(xx, zz):
        b = zz * 4 + xx * 2 + 1 - core
        j = xx * 4 + zz
        return remote(
            gw_ref.at[:, rows(b), :], sib_got.at[j], sib_send.at[j], sib_recv.at[j], (sib, mp)
        )

    def to_across(zz):
        return remote(acc.at[0, zz], x_got.at[zz], x_send.at[zz], x_recv.at[zz], (across, mp))

    def to_up(zz):
        return remote(acc.at[1, zz], up_got.at[zz], z_send.at[0, zz], z_recv.at[0, zz], (dp + 4, mp))

    def to_down(zz):
        return remote(
            acc.at[1, zz], down_got.at[zz], z_send.at[1, zz], z_recv.at[1, zz], (dp - 4, mp)
        )

    half = ga_out.shape[0]
    pair = remote(
        ga_ref.at[pl.ds(pl.multiple_of((1 - mp) * half, half), half), :],
        ga_got,
        ga_send.at[0],
        ga_recv.at[0],
        (dp, 1 - mp),
    )
    lines = pl.ds(pl.multiple_of(mp * layer_ref.shape[1], layer_ref.shape[1]), layer_ref.shape[1])
    swap_layer = remote(
        layer_ref.at[pl.ds(pl.multiple_of((1 - mp) * half, half), half), :],
        layer_out.at[:, lines],
        ga_send.at[1],
        ga_recv.at[1],
        (dp, 1 - mp),
    )
    own_layer = pltpu.make_async_copy(
        layer_ref.at[pl.ds(pl.multiple_of(mp * half, half), half), :],
        layer_out.at[:, lines],
        own_sem,
    )
    for k in range(1, 16):
        scatter(k).start()
    order = (0, 3, 1, 2)
    for zz in order:
        to_sib(1 - x, zz).start()
    for zz in order:
        to_sib(x, zz).start()
    pair.start()
    swap_layer.start()
    own_layer.start()

    def own(b):
        return gw_ref[:, rows(b), :].astype(F32)

    for zz in order:
        to_sib(1 - x, zz).wait_recv()
        b = zz * 4 + (1 - x) * 2 + core
        acc[0, zz] = (own(b) + sib_got[(1 - x) * 4 + zz].astype(F32)).astype(BF)
        to_across(zz).start()
    total = few_ref[dp]
    for k in range(1, 16):
        scatter(k).wait_recv()
        total = total + few_got[k]
    few_part[...] = total
    mate.start()
    for zz in order:
        to_sib(x, zz).wait_recv()
    mate.wait()
    few_total[...] = few_part[...] + few_mate[...]
    few_out[dp] = few_total[...]
    for k in range(1, 16):
        collect(k).start()
    for zz in order:
        to_across(zz).wait_recv()
        b = zz * 4 + x * 2 + core
        part = own(b) + sib_got[x * 4 + zz].astype(F32) + x_got[zz].astype(F32)
        acc[1, zz] = part.astype(BF)

        @pl.when(jnp.logical_and(zz > z, z > 0))
        def _():
            to_up(zz).wait_recv()
            acc[1, zz] = (acc[1, zz].astype(F32) + up_got[zz].astype(F32)).astype(BF)

        @pl.when(jnp.logical_and(zz < z, z < 3))
        def _():
            to_down(zz).wait_recv()
            acc[1, zz] = (acc[1, zz].astype(F32) + down_got[zz].astype(F32)).astype(BF)

        @pl.when(zz > z)
        def _():
            to_up(zz).start()

        @pl.when(zz < z)
        def _():
            to_down(zz).start()

        @pl.when(zz == z)
        def _():
            sum_ref[...] = part

    @pl.when(z > 0)
    def _():
        to_up(z).wait_recv()
        sum_ref[...] += up_got[z].astype(F32)

    @pl.when(z < 3)
    def _():
        to_down(z).wait_recv()
        sum_ref[...] += down_got[z].astype(F32)

    pair.wait()
    swap_layer.wait()
    own_layer.wait()
    ga_out[...] = (
        ga_ref[pl.ds(pl.multiple_of(mp * half, half), half), :].astype(F32)
        + ga_got[...].astype(F32)
    )
    for zz in range(4):
        to_sib(0, zz).wait_send()
        to_sib(1, zz).wait_send()
        to_across(zz).wait_send()

        @pl.when(zz > z)
        def _():
            to_up(zz).wait_send()

        @pl.when(zz < z)
        def _():
            to_down(zz).wait_send()
    for k in range(1, 16):
        scatter(k).wait_send()
        collect(k).wait()


def reduce_weights(gw, ga, layer, arrays):
    kinds, _, width = gw.shape
    block = (kinds, 48, width)
    half = (ga.shape[0] // 2, ga.shape[1])
    flat = jnp.concatenate([a.reshape(-1) for a in arrays])
    rows = -(-flat.size // (16 * 8 * 128)) * 8
    few = jnp.pad(flat, (0, 16 * rows * 128 - flat.size)).reshape(16, rows, 128)
    dma = pltpu.SemaphoreType.DMA
    sums, ga_sum, out, layer_out = pl.pallas_call(
        reduce_kernel,
        out_shape=(
            jax.ShapeDtypeStruct(block, F32),
            jax.ShapeDtypeStruct(half, F32),
            jax.ShapeDtypeStruct(few.shape, F32),
            jax.ShapeDtypeStruct(half, BF),
        ),
        in_specs=[VM] * 4,
        out_specs=[VM] * 4,
        scratch_shapes=[
            pltpu.VMEM((8,) + block, BF),
            pltpu.VMEM((4,) + block, BF),
            pltpu.VMEM((4,) + block, BF),
            pltpu.VMEM((4,) + block, BF),
            pltpu.VMEM((2, 4) + block, BF),
            pltpu.VMEM(half, BF),
            dma((8,)),
            dma((8,)),
            dma((4,)),
            dma((4,)),
            dma((2, 4)),
            dma((2, 4)),
            dma((2,)),
            dma((2,)),
            pltpu.VMEM(few.shape, F32),
            pltpu.VMEM((rows, 128), F32),
            pltpu.VMEM((rows, 128), F32),
            pltpu.VMEM((rows, 128), F32),
            dma((16,)),
            dma((16,)),
            dma((16,)),
            dma((16,)),
            dma,
            dma,
            dma,
        ],
        compiler_params=params(6),
    )(gw, ga, few, layer)
    out = out.reshape(-1)
    ends, at = [], 0
    for a in arrays:
        ends.append(out[at : at + a.size].reshape(a.shape))
        at += a.size
    return sums, ga_sum, ends, layer_out


def local_pairs(
    tokens,
    w_query,
    w_key,
    w_value,
    w_output,
    bias_table,
    gain_attn,
    gain_moe,
    router,
    w_in,
    w_out,
    routes,
    slots,
    buckets,
    cotangent,
):
    length, width = tokens.shape
    half_rows, half = length // 2, width // 2
    mp_rank = lax.axis_index("mp")
    experts = router.shape[1]
    capacity = (5 * length + 4 * experts - 1) // (4 * experts)
    head_width = w_query.shape[1]
    heads = head_width // HEAD_DIM

    def own_rows(array):
        return lax.dynamic_slice_in_dim(array, mp_rank * half_rows, half_rows, 0)

    def own_cols(array):
        return lax.dynamic_slice_in_dim(array, mp_rank * half, half, 1)

    weights = gather_weights(jnp.stack([w_query, w_key, w_value, w_output.T]))
    bucket_hot = (
        buckets[:, None] == jnp.arange(bias_table.shape[0], dtype=jnp.int32)[None, :]
    ).astype(F32)
    bucket_hot = jnp.pad(bucket_hot, ((0, 1), (0, 0)))
    table_heads = lax.dynamic_slice_in_dim(bias_table, mp_rank * heads, heads, 1)
    table_heads = jnp.pad(table_heads, ((0, 0), (0, 8 - heads)))
    offsets = jnp.einsum("ob,bh->ho", bucket_hot, table_heads, precision=lax.Precision.HIGHEST)
    partial, normed_attn, qkv, context, chances = pl.pallas_call(
        lambda *refs: forward_kernel(heads, *refs),
        out_shape=(
            jax.ShapeDtypeStruct((length, width), BF),
            jax.ShapeDtypeStruct((length, width), BF),
            jax.ShapeDtypeStruct((3, length, head_width), BF),
            jax.ShapeDtypeStruct((length, head_width), BF),
            jax.ShapeDtypeStruct((heads, length, length), F32),
        ),
        in_specs=[VM] * 4,
        out_specs=[VM] * 5,
        compiler_params=params(),
    )(tokens, gain_attn[None, :], weights, offsets)
    inputs = tokens.astype(F32)
    residual = inputs + pair_sum(partial)
    moe_float, inverse_moe = normalize(residual, gain_moe)
    normed_moe = moe_float.astype(BF)
    logits = jnp.dot(normed_moe, router, preferred_element_type=F32)
    chance_all = jax.nn.softmax(logits, axis=-1)
    route_hot = (routes[:, None] == jnp.arange(experts, dtype=jnp.int32)[None, :]).astype(F32)
    gates = jnp.sum(chance_all * route_hot, axis=1)
    gradient = cotangent.astype(F32)
    grad_rows = (gates[:, None] * gradient).astype(BF)
    spots = jnp.arange(experts * SLAB, dtype=jnp.int32)[:, None]
    target = (routes * SLAB + slots)[None, :]
    hot_in = (spots == target).astype(BF)
    hot_grad = (spots == target + capacity).astype(BF)
    slab = jnp.dot(
        jnp.concatenate([hot_in, hot_grad], axis=1),
        jnp.concatenate([own_cols(normed_moe), own_cols(grad_rows)], axis=0),
        preferred_element_type=F32,
    ).astype(BF)
    arrived = dispatch(slab.reshape(experts, SLAB, half))
    back_slab, grad_w_in, grad_w_out = expert_layer(arrived, w_in, w_out, capacity)
    returned = combine(back_slab).reshape(experts * SLAB, half)
    expert_rows = dot(hot_in, returned, (0, 0))
    back_half = dot(hot_grad, returned, (0, 0)).astype(BF)
    layer_half = (own_cols(residual) + gates[:, None] * expert_rows).astype(BF)
    gate_half = jnp.sum(own_cols(gradient) * expert_rows, axis=1)
    grad_slots, gate_other = swap(
        back_half, jnp.broadcast_to(gate_half[None, :], (8, length))
    )
    grad_gates = gate_half + gate_other[0]
    grad_logits = (grad_gates[:, None] * gates[:, None] * (route_hot - chance_all)).astype(BF)
    grad_normed = grad_slots.astype(F32) + jnp.einsum(
        "se,de->sd", grad_logits, router, preferred_element_type=F32
    )
    grad_residual = gradient + norm_backward(residual, inverse_moe, gain_moe, grad_normed)
    grad_gain_moe = jnp.sum(own_rows(grad_normed) * own_rows(residual * inverse_moe), axis=0)
    grad_router = jnp.einsum(
        "sd,se->de", own_rows(normed_moe), own_rows(grad_logits), preferred_element_type=F32
    )
    grad_weights, grad_attn, grad_offsets = pl.pallas_call(
        lambda *refs: backward_kernel(heads, *refs),
        out_shape=(
            jax.ShapeDtypeStruct(weights.shape, BF),
            jax.ShapeDtypeStruct((length, width), BF),
            jax.ShapeDtypeStruct((8, 2 * length), F32),
        ),
        in_specs=[VM] * 6,
        out_specs=[VM] * 3,
        scratch_shapes=[
            pltpu.VMEM((length, head_width), BF),
            pltpu.VMEM((3, length, head_width), BF),
        ],
        compiler_params=params(),
    )(grad_residual.astype(BF), normed_attn, weights, qkv, context, chances)
    inverse_attn = lax.rsqrt(jnp.mean(inputs * inputs, axis=-1, keepdims=True) + EPS)
    grad_gain_attn = jnp.sum(grad_attn.astype(F32) * inputs * inverse_attn, axis=0)
    table_part = jnp.einsum(
        "ob,ho->bh", bucket_hot, grad_offsets, precision=lax.Precision.HIGHEST
    )[:, :heads]
    table_full = lax.dynamic_update_slice_in_dim(
        jnp.zeros(bias_table.shape, F32), table_part, mp_rank * heads, 1
    )
    sums, own_grad_attn, few, layer_out = reduce_weights(
        grad_weights,
        grad_attn,
        layer_half,
        [table_full, grad_gain_attn, grad_gain_moe, grad_router],
    )
    grad_table, gain_attn_total, gain_moe_total, router_total = few
    input_grad = own_rows(grad_residual) + norm_backward(
        own_rows(inputs), own_rows(inverse_attn), gain_attn, own_grad_attn
    )
    return (
        layer_out,
        input_grad,
        sums[0],
        sums[1],
        sums[2],
        sums[3].T,
        grad_table,
        gain_attn_total,
        gain_moe_total,
        router_total,
        grad_w_in,
        grad_w_out,
    )


def solution(mesh):
    in_specs = (
        P("dp", None),
        P("dp", "mp"),
        P("dp", "mp"),
        P("dp", "mp"),
        P("mp", "dp"),
        P(),
        P(),
        P(),
        P(),
        P("dp", None, "mp"),
        P("dp", "mp", None),
        P("dp"),
        P("dp"),
        P(),
        P("dp", None),
    )
    out_specs = (
        P(("dp", "mp"), None),
        P(("dp", "mp"), None),
        P("dp", "mp"),
        P("dp", "mp"),
        P("dp", "mp"),
        P("mp", "dp"),
        P(),
        P(),
        P(),
        P(),
        P("dp", None, "mp"),
        P("dp", "mp", None),
    )
    small = mesh.shape["mp"] == 2 and mesh.shape["dp"] == 16
    return jax.shard_map(local_pairs if small else local, mesh=mesh, in_specs=in_specs, out_specs=out_specs, check_vma=False)
```
